256 devices in a mesh: chan: 16 (over z, core), blk: 8 (over y, x_lo), grid: 2 (over x_hi).
Axes of the slice: x: 4 (x_hi: 2, x_lo: 2; x = x_hi * 2 + x_lo), y: 4, z: 8, core: 2. Of those that a mesh axis runs over, the one named last changes fastest.
Arguments:
- samples: bfloat16 [2, 256, 262144], P('grid', 'blk', 'chan'), may hold values from -6 to 6
- pfb_taps: bfloat16 [4, 2048], replicated, may hold values from -0.09375 to 0.09375
- chan_select: int32 [1024], replicated, may hold values from 0 to 1023, each once
Outputs:
- visibility: float32 [2, 1024, 2, 256, 512], P(None, 'chan', None, 'blk', 'grid')
The draws below stay inside these ranges and needn't reach their ends.
Inputs may be any that keep to these rules, and one draw needn't show every extreme that they name: chan_select holds every bin of 0 to 1023 once.
All inputs are finite; a program needn't handle non-finite values.
Results may differ from the reference program's by a relative error of at most 0.0059.
Values may be sent and summed in bfloat16 or wider, within the bound.
A program may use at most 128 MiB of HBM per device.

```python
import math
import jax
import jax.numpy as jnp
from jax import lax

NIN = 512
NCH = 1024
TAPS = 4
FFT = 2048
SPEC = 128
TIME = 262144
N_CHAN = 16
N_GRID = 2


def block_scale(own_key, shape, pieces, low, largest):
    factor_of = 1.0
    for axis_at, parts in pieces:
        steps = jax.random.uniform(jax.random.fold_in(jax.random.fold_in(own_key, 6), axis_at), (parts,), jnp.float32, low / len(pieces), largest / len(pieces))
        factor_of = factor_of * jnp.repeat(jnp.exp(steps), shape[axis_at] // parts).reshape((-1,) + (1,) * (len(shape) - 1 - axis_at))
    return factor_of


def noise(rng, extent, width, limit, shards=(), kind=jnp.bfloat16):
    array = width * jax.random.normal(rng, extent, jnp.float32)
    if shards:
        array = array * block_scale(rng, extent, shards, -0.22, 0.18)
    return jnp.clip(array, -limit, limit).astype(kind)


def setup_inputs(seed: int = 0) -> dict:
    keys = jax.random.split(jax.random.key(seed), 4)
    samples = noise(keys[0], (N_GRID, NIN // N_GRID, TIME), 1.0, 6.0, ((0, 2), (1, 8), (2, 16)))
    pfb_taps = noise(keys[1], (TAPS, FFT), (TAPS * NCH) ** -0.5, 0.09375)
    chan_select = jax.random.permutation(keys[2], NCH).astype(jnp.int32)
    return dict(samples=samples, pfb_taps=pfb_taps, chan_select=chan_select)


def build_dft(chan_select):
    positions = jnp.arange(FFT, dtype=jnp.int32)
    phase_index = (positions[:, None] * chan_select[None, :]) % FFT
    angles = phase_index.astype(jnp.float32) * (2.0 * math.pi / FFT)
    return jnp.stack([jnp.cos(angles), -jnp.sin(angles)], 1).astype(jnp.bfloat16)


def reference(samples, pfb_taps, chan_select):
    frames = samples.reshape(NIN, SPEC, FFT)
    padding = jnp.zeros((NIN, TAPS - 1, FFT), jnp.bfloat16)
    padded = jnp.concatenate([padding, frames], 1)
    filtered = jnp.zeros((NIN, SPEC, FFT), jnp.float32)
    for tap_index in range(TAPS):
        filtered = filtered + pfb_taps[tap_index].astype(jnp.float32) * padded[:, tap_index:tap_index + SPEC].astype(jnp.float32)
    filtered = filtered.astype(jnp.bfloat16)
    dft_table = build_dft(chan_select).reshape(FFT, 2 * NCH)
    spectra = jnp.dot(filtered.reshape(NIN * SPEC, FFT).astype(jnp.float32), dft_table.astype(jnp.float32),
                      precision=lax.Precision.HIGHEST).astype(jnp.bfloat16)
    group_size = NCH // N_CHAN
    spectra = spectra.reshape(NIN, SPEC, 2, N_CHAN, group_size).transpose(3, 0, 1, 2, 4)

    def correlate(block):
        real_part = block[:, :, 0].astype(jnp.float32)
        imag_part = block[:, :, 1].astype(jnp.float32)
        hi = lax.Precision.HIGHEST
        real_vis = jnp.einsum('asc,isc->cai', real_part, real_part, precision=hi) + jnp.einsum('asc,isc->cai', imag_part, imag_part, precision=hi)
        imag_vis = jnp.einsum('asc,isc->cai', imag_part, real_part, precision=hi) - jnp.einsum('asc,isc->cai', real_part, imag_part, precision=hi)
        return jnp.stack([real_vis, imag_vis]) * (1.0 / SPEC)

    groups = lax.map(correlate, spectra)
    visibility = groups.transpose(1, 0, 2, 3, 4).reshape(2, NCH, NIN, NIN)
    return visibility.reshape(2, NCH, N_GRID, NIN // N_GRID, NIN)
```

```python
import math

import jax
import jax.numpy as jnp
from jax import lax
from jax.experimental import pallas as pl
from jax.experimental.pallas import tpu as pltpu
from jax.sharding import PartitionSpec as P

MESH = pl.DeviceIdType.MESH
BF16 = jnp.bfloat16
F32 = jnp.float32
VMEM_LIMIT = 52 * 1024 * 1024

FFT = 2048
TAPS = 4
INPUTS = 32
FRAMES = 8
GROUP = 64
SHARDS = 16
SPECTRA = SHARDS * FRAMES
LANES = 2 * GROUP
HALO = (TAPS - 1) * FFT
COARSE, MIDDLE, FINE = 8, 16, 16
PIECES = 16
PIECE = GROUP // PIECES


def phase_tables(chan_select):
    bins = jnp.broadcast_to(chan_select.reshape(SHARDS, 1, GROUP), (SHARDS, 2, GROUP)).reshape(1, -1)
    quarter = (jnp.arange(SHARDS * LANES, dtype=jnp.int32) // GROUP % 2 * (FFT // 4)).reshape(1, -1)
    rows = jnp.arange(COARSE + MIDDLE + FINE, dtype=jnp.int32).reshape(-1, 1)
    is_coarse = rows < COARSE
    is_middle = rows < COARSE + MIDDLE
    step = jnp.where(is_coarse, rows * 256, jnp.where(is_middle, (rows - COARSE) * 16, rows - COARSE - MIDDLE))
    phase = (step * bins + jnp.where(is_middle, 0, quarter)) % FFT
    angle = phase.astype(F32) * (2.0 * math.pi / FFT)
    return jnp.cos(angle), jnp.sin(angle)


def spectra_kernel(
    samples, taps, cos_ref, sin_ref, out, frames, filt, table, fine_cos, fine_sin, sent, landed,
    spread, turned_re, turned_im, load_sem, halo_sems, send_sems, recv_sems,
):
    me = lax.axis_index("chan")
    my_z, my_core = me // 2, me % 2

    load = pltpu.make_async_copy(samples, frames.at[:, pl.ds(HALO, FRAMES * FFT)], load_sem)
    load.start()

    barrier = pltpu.get_barrier_semaphore()

    def greet(offset, carry):
        pl.semaphore_signal(barrier, inc=1, device_id={"chan": lax.rem(me + offset, SHARDS)}, device_id_type=MESH)
        return carry

    lax.fori_loop(1, SHARDS, greet, 0)
    pl.semaphore_wait(barrier, SHARDS - 1)

    halo = pltpu.make_async_remote_copy(
        src_ref=samples.at[:, pl.ds((FRAMES - TAPS + 1) * FFT, HALO)],
        dst_ref=frames.at[:, pl.ds(0, HALO)],
        send_sem=halo_sems.at[0],
        recv_sem=halo_sems.at[1],
        device_id={"chan": lax.rem(me + 1, SHARDS)},
        device_id_type=MESH,
    )
    halo.start()
    load.wait()

    width = 512

    def filter_frame(s):
        def part(i, carry):
            lanes = pl.multiple_of(i * width, width)
            total = jnp.zeros((INPUTS, width), F32)
            for t in range(TAPS):
                weight = taps[pl.ds(t, 1), pl.ds(lanes, width)].astype(F32)
                total = total + weight * frames[:, pl.ds((s + t) * FFT + lanes, width)].astype(F32)
            filt[pl.ds(s * INPUTS, INPUTS), pl.ds(lanes, width)] = total.astype(BF16)
            return carry

        lax.fori_loop(0, FFT // width, part, 0)

    for s in range(TAPS - 1, FRAMES):
        filter_frame(s)

    halo.wait_send()
    halo.wait_recv()

    @pl.when(me == 0)
    def _():
        frames[:, pl.ds(0, HALO)] = jnp.zeros((INPUTS, HALO), BF16)

    for s in range(TAPS - 1):
        filter_frame(s)

    def send(group):
        return pltpu.make_async_remote_copy(
            src_ref=sent.at[group],
            dst_ref=landed.at[me],
            send_sem=send_sems.at[group],
            recv_sem=recv_sems.at[me],
            device_id={"chan": group},
            device_id_type=MESH,
        )

    def transform(i, carry):
        away = 4 + (i + 1) // 2 * (1 - 2 * (i % 2))
        to_z = lax.rem(my_z + away, SHARDS // 2)
        lanes = pl.ds(pl.multiple_of(to_z * 2 * LANES, 2 * LANES), 2 * LANES)
        for u in range(MIDDLE):
            cos_u, sin_u = cos_ref[pl.ds(COARSE + u, 1), lanes], sin_ref[pl.ds(COARSE + u, 1), lanes]
            cos_v = cos_ref[pl.ds(COARSE + MIDDLE, FINE), lanes]
            sin_v = sin_ref[pl.ds(COARSE + MIDDLE, FINE), lanes]
            fine_cos[pl.ds(u * FINE, FINE), :] = cos_u * cos_v - sin_u * sin_v
            fine_sin[pl.ds(u * FINE, FINE), :] = sin_u * cos_v + cos_u * sin_v
        for p in range(COARSE):
            cos_p, sin_p = cos_ref[pl.ds(p, 1), lanes], sin_ref[pl.ds(p, 1), lanes]
            table[pl.ds(p * 256, 256), :] = (cos_p * fine_cos[...] - sin_p * fine_sin[...]).astype(BF16)
        spectra = jnp.dot(filt[...], table[...], preferred_element_type=F32).astype(BF16)
        for core in range(2):
            group = to_z * 2 + core
            sent[group] = spectra[:, core * LANES : (core + 1) * LANES]

            @pl.when(group != me)
            def _():
                send(group).start()

        return carry

    lax.fori_loop(0, SHARDS // 2, transform, 0)

    def widen(shard, source):
        rows = pl.ds(pl.multiple_of(shard * FRAMES * INPUTS, FRAMES * INPUTS), FRAMES * INPUTS)
        spread[rows, :] = source.astype(F32)

    widen(me, sent[me])

    def arrive(i, carry):
        half = (i + 1) // 2
        shard = lax.rem(me + SHARDS + half * (1 - 2 * (i % 2)), SHARDS)
        pltpu.make_async_remote_copy(
            src_ref=sent.at[shard], dst_ref=landed.at[shard], send_sem=send_sems.at[shard],
            recv_sem=recv_sems.at[shard], device_id={"chan": shard}, device_id_type=MESH,
        ).wait_recv()
        widen(shard, landed[shard])
        return carry

    lax.fori_loop(1, SHARDS, arrive, 0)

    def turn(a, carry):
        block = spread[pl.ds(a, SPECTRA, stride=INPUTS), :].T
        turned_re[pl.ds(a, GROUP, stride=INPUTS), :] = block[:GROUP]
        turned_im[pl.ds(a, GROUP, stride=INPUTS), :] = block[GROUP:]
        return carry

    lax.fori_loop(0, INPUTS, turn, 0)

    def narrow(c, carry):
        rows = pl.ds(pl.multiple_of(c * INPUTS, INPUTS), INPUTS)
        out[c, :, pl.ds(0, SPECTRA)] = turned_re[rows, :].astype(BF16)
        out[c, :, pl.ds(SPECTRA, SPECTRA)] = turned_im[rows, :].astype(BF16)
        return carry

    lax.fori_loop(0, GROUP, narrow, 0)

    def drain(offset, carry):
        send(lax.rem(me + offset, SHARDS)).wait_send()
        return carry

    lax.fori_loop(1, SHARDS, drain, 0)


def turned_spectra(samples, taps, cos_table, sin_table):
    vmem = pl.BlockSpec(memory_space=pltpu.VMEM)
    rows = FRAMES * INPUTS
    return pl.pallas_call(
        spectra_kernel,
        out_shape=jax.ShapeDtypeStruct((GROUP, INPUTS, 2 * SPECTRA), BF16),
        in_specs=[pl.BlockSpec(memory_space=pl.ANY), vmem, vmem, vmem],
        out_specs=vmem,
        scratch_shapes=[
            pltpu.VMEM((INPUTS, HALO + FRAMES * FFT), BF16),
            pltpu.VMEM((rows, FFT), BF16),
            pltpu.VMEM((FFT, 2 * LANES), BF16),
            pltpu.VMEM((256, 2 * LANES), F32),
            pltpu.VMEM((256, 2 * LANES), F32),
            pltpu.VMEM((SHARDS, rows, LANES), BF16),
            pltpu.VMEM((SHARDS, rows, LANES), BF16),
            pltpu.VMEM((SPECTRA * INPUTS, LANES), F32),
            pltpu.VMEM((GROUP * INPUTS, SPECTRA), F32),
            pltpu.VMEM((GROUP * INPUTS, SPECTRA), F32),
            pltpu.SemaphoreType.DMA,
            pltpu.SemaphoreType.DMA((2,)),
            pltpu.SemaphoreType.DMA((SHARDS,)),
            pltpu.SemaphoreType.DMA((SHARDS,)),
        ],
        compiler_params=pltpu.CompilerParams(
            collective_id=0, has_side_effects=True, vmem_limit_bytes=VMEM_LIMIT
        ),
        name="spectra",
    )(samples, taps, cos_table, sin_table)


PAIR, UP, DOWN, FAR, PAIR_UP, PAIR_DOWN, PAIR_FAR, ROW = range(8)


def gather_kernel(own, columns, rows, local_sem, send_sems, recv_sems):
    blk = lax.axis_index("blk")
    grid = lax.axis_index("grid")
    y, x = blk // 2, blk % 2

    def at(y_to, x_to):
        return lax.rem(y_to, 4) * 2 + x_to

    pair = at(y, 1 - x)
    below, above, far = at(y + 3, x), at(y + 1, x), at(y + 2, x)
    pair_below, pair_above, pair_far = at(y + 3, 1 - x), at(y + 1, 1 - x), at(y + 2, 1 - x)
    across = {"blk": pair, "grid": 1 - grid}

    barrier = pltpu.get_barrier_semaphore()
    for partner in ({"blk": pair}, {"blk": below}, {"blk": above}, across):
        pl.semaphore_signal(barrier, inc=1, device_id=partner, device_id_type=MESH)
    pl.semaphore_wait(barrier, 4)

    def piece(i, count=1):
        return pl.ds(i * PIECE, PIECE * count)

    def copy(kind, i, source, slot, partner):
        target = rows.at[piece(i)] if kind == ROW else columns.at[slot, piece(i)]
        return pltpu.make_async_remote_copy(
            src_ref=source, dst_ref=target, send_sem=send_sems.at[kind], recv_sem=recv_sems.at[kind, i],
            device_id=partner, device_id_type=MESH,
        )

    def held(slot, i):
        return columns.at[slot, piece(i)]

    def arrived(kind, i):
        copy(kind, i, own.at[piece(i)], blk, {"blk": pair}).wait_recv()

    keep = pltpu.make_async_copy(own, columns.at[blk], local_sem)
    keep.start()

    def first(i, carry):
        mine = own.at[piece(i)]
        copy(PAIR, i, mine, blk, {"blk": pair}).start()
        copy(UP, i, mine, blk, {"blk": above}).start()
        copy(DOWN, i, mine, blk, {"blk": below}).start()
        return carry

    lax.fori_loop(0, PIECES, first, 0)

    def second(j, carry):
        i = 2 * j
        arrived(PAIR, i)
        copy(ROW, i, held(pair, i), pair, across).start()
        copy(PAIR_UP, i, held(pair, i), pair, {"blk": above}).start()
        copy(PAIR_DOWN, i, held(pair, i), pair, {"blk": below}).start()
        arrived(UP, i)
        copy(FAR, i, held(below, i), below, {"blk": above}).start()
        arrived(DOWN, i)
        k = i + 1
        arrived(UP, k)
        copy(PAIR_UP, k, held(below, k), below, {"blk": pair}).start()
        arrived(DOWN, k)
        copy(FAR, k, held(above, k), above, {"blk": below}).start()
        copy(PAIR_DOWN, k, held(above, k), above, {"blk": pair}).start()
        arrived(PAIR, k)
        copy(ROW, k, held(pair, k), pair, across).start()
        return carry

    lax.fori_loop(0, PIECES // 2, second, 0)

    def third(j, carry):
        i = 2 * j
        k = i + 1
        arrived(FAR, k)
        copy(PAIR_FAR, k, held(far, k), far, {"blk": pair}).start()
        arrived(FAR, i)
        arrived(PAIR_UP, i)
        arrived(PAIR_DOWN, i)

        @pl.when(j % 2 == 0)
        def _():
            copy(PAIR_FAR, i, held(pair_below, i), pair_below, {"blk": above}).start()

        @pl.when(j % 2 == 1)
        def _():
            copy(PAIR_FAR, i, held(pair_above, i), pair_above, {"blk": below}).start()

        return carry

    lax.fori_loop(0, PIECES // 2, third, 0)

    def fourth(j, carry):
        i = 2 * j
        k = i + 1
        arrived(PAIR_UP, k)
        arrived(PAIR_DOWN, k)
        arrived(PAIR_FAR, i)
        arrived(PAIR_FAR, k)
        arrived(ROW, i)
        arrived(ROW, k)
        return carry

    lax.fori_loop(0, PIECES // 2, fourth, 0)
    keep.wait()
    for kind in range(8):
        pltpu.make_async_remote_copy(
            src_ref=own, dst_ref=rows, send_sem=send_sems.at[kind], recv_sem=recv_sems.at[kind, 0],
            device_id={"blk": pair}, device_id_type=MESH,
        ).wait_send()


def gathered_spectra(own):
    anywhere = pl.BlockSpec(memory_space=pl.ANY)
    return pl.pallas_call(
        gather_kernel,
        out_shape=[
            jax.ShapeDtypeStruct((8,) + own.shape, BF16),
            jax.ShapeDtypeStruct(own.shape, BF16),
        ],
        in_specs=[anywhere],
        out_specs=[anywhere, anywhere],
        scratch_shapes=[
            pltpu.SemaphoreType.DMA,
            pltpu.SemaphoreType.DMA((8,)),
            pltpu.SemaphoreType.DMA((8, PIECES)),
        ],
        compiler_params=pltpu.CompilerParams(
            collective_id=1, has_side_effects=True, vmem_limit_bytes=VMEM_LIMIT
        ),
        name="gather",
    )(own)


CHANNELS = 8


def cross_kernel(first, second, columns, out):
    for c in range(CHANNELS):
        left = jnp.concatenate([first[c], second[c]], 0)
        quarter = jnp.concatenate([left[:, SPECTRA:], -left[:, :SPECTRA]], 1)
        right = columns[:, c].reshape(8 * INPUTS, 2 * SPECTRA)
        product = lax.dot_general(
            jnp.concatenate([left, quarter], 0), right, (((1,), (1,)), ((), ())), preferred_element_type=F32
        ) * (1.0 / SPECTRA)
        out[:, c] = product.reshape(2, 2, INPUTS, 8 * INPUTS)


def cross_products(first, second, columns):
    shape = (2, GROUP, 2, INPUTS, 8 * INPUTS)
    block = pl.BlockSpec((CHANNELS, INPUTS, 2 * SPECTRA), lambda i: (i, 0, 0))
    return pl.pallas_call(
        cross_kernel,
        grid=(GROUP // CHANNELS,),
        out_shape=jax.ShapeDtypeStruct(shape, F32),
        in_specs=[block, block, pl.BlockSpec((8, CHANNELS, INPUTS, 2 * SPECTRA), lambda i: (0, i, 0, 0))],
        out_specs=pl.BlockSpec((2, CHANNELS, 2, INPUTS, 8 * INPUTS), lambda i: (0, i, 0, 0, 0)),
        compiler_params=pltpu.CompilerParams(vmem_limit_bytes=VMEM_LIMIT),
        name="cross",
    )(first, second, columns)


def body(samples, pfb_taps, chan_select):
    cos_table, sin_table = phase_tables(chan_select)
    own = turned_spectra(samples[0], pfb_taps, cos_table, sin_table)
    columns, other = gathered_spectra(own)
    lower = lax.axis_index("grid") == 0
    return cross_products(jnp.where(lower, own, other), jnp.where(lower, other, own), columns)


def solution(mesh):
    return jax.shard_map(
        body,
        mesh=mesh,
        in_specs=(P("grid", "blk", "chan"), P(), P()),
        out_specs=P(None, "chan", None, "blk", "grid"),
        check_vma=False,
    )
```

```python
import math

import jax
import jax.numpy as jnp
from jax import lax
from jax.experimental import pallas as pl
from jax.experimental.pallas import tpu as pltpu
from jax.sharding import PartitionSpec as P

MESH = pl.DeviceIdType.MESH
BF16 = jnp.bfloat16
F32 = jnp.float32
VMEM_LIMIT = 22 * 1024 * 1024
CROSS_LIMIT = 24 * 1024 * 1024

FFT = 2048
TAPS = 4
INPUTS = 32
FRAMES = 8
GROUP = 64
SHARDS = 16
SPECTRA = SHARDS * FRAMES
LANES = 2 * GROUP
HALO = (TAPS - 1) * FFT
COARSE, MIDDLE, FINE = 8, 16, 16

PARTS = 4
STEPS = FRAMES // 2
PART = INPUTS // 2
HEIGHT = STEPS * PART
DEPTH = SHARDS * STEPS
BLOCK = (PARTS, GROUP, PART, 2 * DEPTH)
PIECES = ((0, 18), (18, 18), (36, 14), (50, 14))
PAIR, UP, DOWN, FAR, PAIR_UP, PAIR_DOWN, PAIR_FAR, ROW = range(8)


def cos_sin(phase):
    turns = (phase + FFT // 8) // (FFT // 4)
    angle = (phase - turns * (FFT // 4)).astype(F32) * (2.0 * math.pi / FFT)
    square = angle * angle
    cosine = 1.0 + square * (-1.0 / 2 + square * (1.0 / 24 + square * (-1.0 / 720 + square * (1.0 / 40320))))
    sine = angle * (1.0 + square * (-1.0 / 6 + square * (1.0 / 120 + square * (-1.0 / 5040 + square * (1.0 / 362880)))))
    odd = turns % 2 == 1
    out_cos = jnp.where(odd, sine, cosine)
    out_sin = jnp.where(odd, cosine, sine)
    return (
        jnp.where((turns == 1) | (turns == 2), -out_cos, out_cos),
        jnp.where((turns == 2) | (turns == 3), -out_sin, out_sin),
    )


def spectra_kernel(
    samples, taps, chan_select, columns, rows, history, filt, table, fine_cos, fine_sin, sent, landed,
    spread, turned, own, halo_sems, turn_send, turn_recv, keep_sems, send_sems, recv_sems,
):
    me = lax.axis_index("chan")
    blk = lax.axis_index("blk")
    grid = lax.axis_index("grid")
    my_z = me // 2
    y, x = blk // 2, blk % 2

    def at(y_to, x_to):
        return lax.rem(y_to, 4) * 2 + x_to

    pair = at(y, 1 - x)
    below, above, far = at(y + 3, x), at(y + 1, x), at(y + 2, x)
    pair_below, pair_above = at(y + 3, 1 - x), at(y + 1, 1 - x)
    to_pair, to_below, to_above = {"blk": pair}, {"blk": below}, {"blk": above}
    to_across = {"blk": pair, "grid": 1 - grid}

    barrier = pltpu.get_barrier_semaphore()

    def greet(offset, carry):
        pl.semaphore_signal(barrier, inc=1, device_id={"chan": lax.rem(me + offset, SHARDS)}, device_id_type=MESH)
        return carry

    lax.fori_loop(1, SHARDS, greet, 0)
    for partner in (to_pair, to_below, to_above, to_across):
        pl.semaphore_signal(barrier, inc=1, device_id=partner, device_id_type=MESH)

    width = 512

    def filter_frames(early):
        for step in range(STEPS):
            s = step + STEPS * (1 - early)

            def part(i, carry):
                lanes = pl.multiple_of(i * width, width)
                total = jnp.zeros((INPUTS, width), F32)
                for t in range(TAPS):
                    weight = taps[pl.ds(t, 1), pl.ds(lanes, width)].astype(F32)
                    frame = s + t - (TAPS - 1)
                    if frame < 0:
                        source = history[:, pl.ds((s + t) * FFT + lanes, width)]
                    else:
                        source = samples[:, pl.ds(frame * FFT + lanes, width)]
                    total = total + weight * source.astype(F32)
                total = total.astype(BF16)
                for half in range(2):
                    place = pl.ds(((2 * early + half) * STEPS + step) * PART, PART)
                    filt[place, pl.ds(lanes, width)] = total[half * PART : (half + 1) * PART]
                return carry

            lax.fori_loop(0, FFT // width, part, 0)

    filter_frames(0)
    pl.semaphore_wait(barrier, SHARDS - 1 + 4)

    def send(part, group):
        return pltpu.make_async_remote_copy(
            src_ref=sent.at[part, group],
            dst_ref=landed.at[part, me],
            send_sem=turn_send.at[part, group],
            recv_sem=turn_recv.at[part, me],
            device_id={"chan": group},
            device_id_type=MESH,
        )

    def chip(i):
        away = 4 + (i + 1) // 2 * (1 - 2 * (i % 2))
        return lax.rem(my_z + away, SHARDS // 2)

    def leave(part, group):
        @pl.when(group != me)
        def _():
            send(part, group).start()

    def leave_later(part):
        def step(i, carry):
            for core in range(2):
                leave(part, chip(i) * 2 + core)
            return carry

        lax.fori_loop(0, SHARDS // 2, step, 0)

    def build_table(to_z):
        bins = jnp.broadcast_to(chan_select[pl.ds(to_z, 1), :], (8, LANES))
        other = pltpu.roll(bins, GROUP, 1)
        low = lax.broadcasted_iota(jnp.int32, (8, LANES), 1) < GROUP
        bins = jnp.concatenate([jnp.where(low, bins, other), jnp.where(low, other, bins)], 1)
        quarter = jnp.where(low, 0, FFT // 4)
        quarter = jnp.concatenate([quarter, quarter], 1)
        row = lax.broadcasted_iota(jnp.int32, (8, 2 * LANES), 0)
        cos_p, sin_p = cos_sin(row * 256 * bins % FFT)
        middle = [cos_sin((row + 8 * k) * 16 * bins % FFT) for k in range(MIDDLE // 8)]
        fine = [cos_sin(((row + 8 * k) * bins + quarter) % FFT) for k in range(FINE // 8)]
        cos_v = jnp.concatenate([both[0] for both in fine], 0)
        sin_v = jnp.concatenate([both[1] for both in fine], 0)
        for u in range(MIDDLE):
            cos_u, sin_u = (t[u % 8 : u % 8 + 1] for t in middle[u // 8])
            fine_cos[pl.ds(u * FINE, FINE), :] = cos_u * cos_v - sin_u * sin_v
            fine_sin[pl.ds(u * FINE, FINE), :] = sin_u * cos_v + cos_u * sin_v
        for p in range(COARSE):
            place = pl.ds(p * 256, 256)
            turned_on = cos_p[p : p + 1] * fine_cos[...] - sin_p[p : p + 1] * fine_sin[...]
            table[to_z, place, :] = turned_on.astype(BF16)

    def transform(early, to_z):
        spectra = jnp.dot(filt[pl.ds(early * 2 * HEIGHT, 2 * HEIGHT), :], table[to_z], preferred_element_type=F32)
        spectra = spectra.astype(BF16)
        for core in range(2):
            for half in range(2):
                sent[2 * early + half, to_z * 2 + core] = spectra[
                    half * HEIGHT : (half + 1) * HEIGHT, core * LANES : (core + 1) * LANES
                ]

    def later_frames(i, carry):
        to_z = chip(i)
        build_table(to_z)
        transform(0, to_z)
        for core in range(2):
            leave(0, to_z * 2 + core)
        return carry

    lax.fori_loop(0, SHARDS // 2, later_frames, 0)

    halo = pltpu.make_async_remote_copy(
        src_ref=samples.at[:, pl.ds((FRAMES - TAPS + 1) * FFT, HALO)],
        dst_ref=history,
        send_sem=halo_sems.at[0],
        recv_sem=halo_sems.at[1],
        device_id={"chan": lax.rem(me + 1, SHARDS)},
        device_id_type=MESH,
    )
    halo.start()
    leave_later(1)

    def early_frames():
        halo.wait_send()
        halo.wait_recv()

        @pl.when(me == 0)
        def _():
            history[...] = jnp.zeros((INPUTS, HALO), BF16)

        filter_frames(1)

        def step(i, carry):
            to_z = chip(i)
            transform(1, to_z)
            for core in range(2):
                leave(2, to_z * 2 + core)
            return carry

        lax.fori_loop(0, SHARDS // 2, step, 0)
        leave_later(3)

    def widen(shard, source):
        spread[pl.ds(pl.multiple_of(shard * HEIGHT, HEIGHT), HEIGHT), :] = source.astype(F32)

    def turn_part(part):
        widen(me, sent[part, me])

        def arrive(i, carry):
            shard = lax.rem(me + SHARDS + (i + 1) // 2 * (1 - 2 * (i % 2)), SHARDS)
            pltpu.make_async_remote_copy(
                src_ref=sent.at[part, shard], dst_ref=landed.at[part, shard], send_sem=turn_send.at[part, shard],
                recv_sem=turn_recv.at[part, shard], device_id={"chan": shard}, device_id_type=MESH,
            ).wait_recv()
            widen(shard, landed[part, shard])
            return carry

        lax.fori_loop(1, SHARDS, arrive, 0)
        low = lax.broadcasted_iota(jnp.int32, (GROUP, 2 * DEPTH), 1) < DEPTH

        def turn(k, carry):
            for j in range(2):
                a = 4 * k + 2 * j
                both = jnp.concatenate([spread[pl.ds(a + b, DEPTH, stride=PART), :] for b in range(2)], 0).T
                real, imag = both[:GROUP], both[GROUP:]
                turned[pl.ds(a, GROUP, stride=PART), :] = jnp.where(low, real, pltpu.roll(imag, DEPTH, 1))
                turned[pl.ds(a + 1, GROUP, stride=PART), :] = jnp.where(low, pltpu.roll(real, DEPTH, 1), imag)
            return carry

        lax.fori_loop(0, PART // 4, turn, 0)

        def narrow(c, carry):
            place = pl.ds(pl.multiple_of(c * 8 * PART, 8 * PART), 8 * PART)
            own[part, pl.ds(c * 8, 8)] = turned[place, :].astype(BF16).reshape(8, PART, 2 * DEPTH)
            return carry

        lax.fori_loop(0, GROUP // 8, narrow, 0)

    def copy(kind, part, i, partner):
        channels = pl.ds(*PIECES[i])
        return pltpu.make_async_remote_copy(
            src_ref=own.at[part, channels], dst_ref=columns.at[blk, part, channels],
            send_sem=send_sems.at[kind, part], recv_sem=recv_sems.at[kind, part, i],
            device_id=partner, device_id_type=MESH,
        )

    def arrived(kind, part, i):
        copy(kind, part, i, to_pair).wait_recv()

    def keep(part):
        return [
            pltpu.make_async_copy(own.at[part], columns.at[blk, part], keep_sems.at[0, part]),
            pltpu.make_async_copy(own.at[part], rows.at[grid, part], keep_sems.at[1, part]),
        ]

    def first(part):
        for i in (0, 2, 1, 3):
            copy(PAIR, part, i, to_pair).start()
            copy(UP, part, i, to_above).start()
            copy(DOWN, part, i, to_below).start()
        for local in keep(part):
            local.start()

    def pass_on(kind, part, i, slot, partner):
        channels = pl.ds(*PIECES[i])
        target = rows.at[grid, part, channels] if kind == ROW else columns.at[slot, part, channels]
        pltpu.make_async_remote_copy(
            src_ref=columns.at[slot, part, channels], dst_ref=target,
            send_sem=send_sems.at[kind, part], recv_sem=recv_sems.at[kind, part, i],
            device_id=partner, device_id_type=MESH,
        ).start()

    def pass_far(part, i):
        if i % 2 == 0:
            pass_on(FAR, part, i, below, to_above)
        else:
            pass_on(FAR, part, i, above, to_below)

    def second(part):
        for i in (0, 2, 1, 3):
            arrived(PAIR, part, i)
            arrived(UP, part, i)
            arrived(DOWN, part, i)
            if i < 2:
                pass_on(PAIR_UP, part, i, pair, to_above)
                pass_on(PAIR_DOWN, part, i, pair, to_below)
            else:
                pass_on(PAIR_UP, part, i, below, to_pair)
                pass_on(PAIR_DOWN, part, i, above, to_pair)
            pass_far(part, i)
            pass_on(ROW, part, i, pair, to_across)

    def third(part):
        for i in (2, 0, 3, 1):
            arrived(FAR, part, i)
            if i >= 2:
                pass_on(PAIR_FAR, part, i, far, to_pair)
            else:
                arrived(PAIR_UP, part, i)
                arrived(PAIR_DOWN, part, i)
                if i == 0:
                    pass_on(PAIR_FAR, part, i, pair_below, to_above)
                else:
                    pass_on(PAIR_FAR, part, i, pair_above, to_below)

    def fourth(part):
        for i in (2, 3):
            arrived(PAIR_UP, part, i)
            arrived(PAIR_DOWN, part, i)
        for i in range(4):
            arrived(PAIR_FAR, part, i)
            arrived(ROW, part, i)

    turn_part(0)
    first(0)
    early_frames()
    turn_part(1)
    first(1)
    second(0)
    turn_part(2)
    first(2)
    second(1)
    third(0)
    turn_part(3)
    first(3)
    second(2)
    third(1)
    second(3)
    third(2)
    third(3)
    for part in range(PARTS):
        fourth(part)
    for part in range(PARTS):
        for local in keep(part):
            local.wait()
        for kind in range(8):
            pltpu.make_async_remote_copy(
                src_ref=own.at[part], dst_ref=columns.at[0, part], send_sem=send_sems.at[kind, part],
                recv_sem=recv_sems.at[kind, part, 0], device_id=to_pair, device_id_type=MESH,
            ).wait_send()

    def drain(offset, carry):
        for part in range(PARTS):
            send(part, lax.rem(me + offset, SHARDS)).wait_send()
        return carry

    lax.fori_loop(1, SHARDS, drain, 0)


def gathered_spectra(samples, taps, chan_select):
    vmem = pl.BlockSpec(memory_space=pltpu.VMEM)
    anywhere = pl.BlockSpec(memory_space=pl.ANY)
    return pl.pallas_call(
        spectra_kernel,
        out_shape=[
            jax.ShapeDtypeStruct((8,) + BLOCK, BF16),
            jax.ShapeDtypeStruct((2,) + BLOCK, BF16),
        ],
        in_specs=[vmem, vmem, vmem],
        out_specs=[anywhere, anywhere],
        scratch_shapes=[
            pltpu.VMEM((INPUTS, HALO), BF16),
            pltpu.VMEM((PARTS * HEIGHT, FFT), BF16),
            pltpu.VMEM((SHARDS // 2, FFT, 2 * LANES), BF16),
            pltpu.VMEM((256, 2 * LANES), F32),
            pltpu.VMEM((256, 2 * LANES), F32),
            pltpu.VMEM((PARTS, SHARDS, HEIGHT, LANES), BF16),
            pltpu.VMEM((PARTS, SHARDS, HEIGHT, LANES), BF16),
            pltpu.VMEM((SHARDS * HEIGHT, LANES), F32),
            pltpu.VMEM((GROUP * PART, 2 * DEPTH), F32),
            pltpu.VMEM(BLOCK, BF16),
            pltpu.SemaphoreType.DMA((2,)),
            pltpu.SemaphoreType.DMA((PARTS, SHARDS)),
            pltpu.SemaphoreType.DMA((PARTS, SHARDS)),
            pltpu.SemaphoreType.DMA((2, PARTS)),
            pltpu.SemaphoreType.DMA((8, PARTS)),
            pltpu.SemaphoreType.DMA((8, PARTS, len(PIECES))),
        ],
        compiler_params=pltpu.CompilerParams(
            collective_id=0, has_side_effects=True, vmem_limit_bytes=VMEM_LIMIT
        ),
        name="spectra",
    )(samples, taps, chan_select)


CHANNELS = 8
CHUNKS = GROUP // CHANNELS


def cross_kernel(rows, columns, out, products, out_sems):
    sign = jnp.where(lax.broadcasted_iota(jnp.int32, (2 * INPUTS, 2 * DEPTH), 1) < DEPTH, 1.0, -1.0).astype(BF16)

    def store(i):
        channels = pl.ds(i * CHANNELS, CHANNELS)
        return pltpu.make_async_copy(products.at[:, channels], out.at[:, channels], out_sems.at[i])

    def operand(data, c):
        early_and_late = []
        for early in range(2):
            halves = [data[:, 2 * early + half, c] for half in range(2)]
            early_and_late.append(jnp.stack(halves, 1).reshape(-1, 2 * DEPTH))
        return early_and_late

    def multiply(i, carry):
        for j in range(CHANNELS):
            c = i * CHANNELS + j
            left = operand(rows, c)
            quarter = [jnp.concatenate([block[:, DEPTH:], block[:, :DEPTH]], 1) * sign for block in left]
            left = jnp.concatenate([jnp.concatenate(left, 1), jnp.concatenate(quarter, 1)], 0)
            product = lax.dot_general(
                left, jnp.concatenate(operand(columns, c), 1), (((1,), (1,)), ((), ())),
                preferred_element_type=F32,
            ) * (1.0 / SPECTRA)
            products[:, c] = product.reshape(2, 2, INPUTS, 8 * INPUTS)
        store(i).start()
        return carry

    lax.fori_loop(0, CHUNKS, multiply, 0)

    def finish(i, carry):
        store(i).wait()
        return carry

    lax.fori_loop(0, CHUNKS, finish, 0)


def cross_products(rows, columns):
    shape = (2, GROUP, 2, INPUTS, 8 * INPUTS)
    return pl.pallas_call(
        cross_kernel,
        out_shape=jax.ShapeDtypeStruct(shape, F32),
        in_specs=[pl.BlockSpec(memory_space=pltpu.VMEM)] * 2,
        out_specs=pl.BlockSpec(memory_space=pltpu.HBM),
        scratch_shapes=[pltpu.VMEM(shape, F32), pltpu.SemaphoreType.DMA((CHUNKS,))],
        compiler_params=pltpu.CompilerParams(vmem_limit_bytes=CROSS_LIMIT),
        name="cross",
    )(rows, columns)


def body(samples, pfb_taps, chan_select):
    columns, rows = gathered_spectra(samples[0], pfb_taps, chan_select.reshape(SHARDS // 2, LANES))
    return cross_products(rows, columns)


def solution(mesh):
    return jax.shard_map(
        body,
        mesh=mesh,
        in_specs=(P("grid", "blk", "chan"), P(), P()),
        out_specs=P(None, "chan", None, "blk", "grid"),
        check_vma=False,
    )
```

```python
import math

import jax
import jax.numpy as jnp
from jax import lax
from jax.experimental import pallas as pl
from jax.experimental.pallas import tpu as pltpu
from jax.sharding import PartitionSpec as P

MESH = pl.DeviceIdType.MESH
BF16 = jnp.bfloat16
F32 = jnp.float32
VMEM_LIMIT = 22 * 1024 * 1024
CROSS_LIMIT = 24 * 1024 * 1024

FFT = 2048
TAPS = 4
INPUTS = 32
FRAMES = 8
GROUP = 64
SHARDS = 16
SPECTRA = SHARDS * FRAMES
LANES = 2 * GROUP
HALO = (TAPS - 1) * FFT
COARSE, MIDDLE, FINE = 8, 16, 16

PARTS = 4
STEPS = FRAMES // 2
PART = INPUTS // 2
HEIGHT = STEPS * PART
DEPTH = SHARDS * STEPS
BLOCK = (PARTS, GROUP, PART, 2 * DEPTH)
SPLIT = 36
PAIR, UP, DOWN, FAR, PAIR_UP, PAIR_DOWN, PAIR_FAR, ROW = range(8)


def cos_sin(phase):
    turns = (phase + FFT // 8) // (FFT // 4)
    angle = (phase - turns * (FFT // 4)).astype(F32) * (2.0 * math.pi / FFT)
    square = angle * angle
    cosine = 1.0 + square * (-1.0 / 2 + square * (1.0 / 24 + square * (-1.0 / 720 + square * (1.0 / 40320))))
    sine = angle * (1.0 + square * (-1.0 / 6 + square * (1.0 / 120 + square * (-1.0 / 5040 + square * (1.0 / 362880)))))
    odd = turns % 2 == 1
    out_cos = jnp.where(odd, sine, cosine)
    out_sin = jnp.where(odd, cosine, sine)
    return (
        jnp.where((turns == 1) | (turns == 2), -out_cos, out_cos),
        jnp.where((turns == 2) | (turns == 3), -out_sin, out_sin),
    )


def spectra_kernel(
    samples, taps, chan_select, columns, rows, history, filt, fine_cos, fine_sin, sent, landed,
    spread, turned, own, halo_sems, turn_send, turn_recv, keep_sems, send_sems, recv_sems, *tables,
):
    me = lax.axis_index("chan")
    blk = lax.axis_index("blk")
    grid = lax.axis_index("grid")
    my_z = me // 2
    y, x = blk // 2, blk % 2

    def at(y_to, x_to):
        return lax.rem(y_to, 4) * 2 + x_to

    pair = at(y, 1 - x)
    below, above, far = at(y + 3, x), at(y + 1, x), at(y + 2, x)
    pair_below, pair_above = at(y + 3, 1 - x), at(y + 1, 1 - x)
    to_pair, to_below, to_above = {"blk": pair}, {"blk": below}, {"blk": above}
    to_across = {"blk": pair, "grid": 1 - grid}

    barrier = pltpu.get_barrier_semaphore()

    def greet(offset, carry):
        pl.semaphore_signal(barrier, inc=1, device_id={"chan": lax.rem(me + offset, SHARDS)}, device_id_type=MESH)
        return carry

    lax.fori_loop(1, SHARDS, greet, 0)
    for partner in (to_pair, to_below, to_above, to_across):
        pl.semaphore_signal(barrier, inc=1, device_id=partner, device_id_type=MESH)

    width = 512

    def filter_frames(early):
        for step in range(STEPS):
            s = step + STEPS * (1 - early)

            def part(i, carry):
                lanes = pl.multiple_of(i * width, width)
                total = jnp.zeros((INPUTS, width), F32)
                for t in range(TAPS):
                    weight = taps[pl.ds(t, 1), pl.ds(lanes, width)].astype(F32)
                    frame = s + t - (TAPS - 1)
                    if frame < 0:
                        source = history[:, pl.ds((s + t) * FFT + lanes, width)]
                    else:
                        source = samples[:, pl.ds(frame * FFT + lanes, width)]
                    total = total + weight * source.astype(F32)
                total = total.astype(BF16)
                for half in range(2):
                    place = pl.ds(((2 * early + half) * STEPS + step) * PART, PART)
                    filt[place, pl.ds(lanes, width)] = total[half * PART : (half + 1) * PART]
                return carry

            lax.fori_loop(0, FFT // width, part, 0)

    filter_frames(0)
    pl.semaphore_wait(barrier, SHARDS - 1 + 4)

    def send(part, group):
        pltpu.make_async_remote_copy(
            src_ref=sent.at[part, group],
            dst_ref=landed.at[part, me],
            send_sem=turn_send.at[part],
            recv_sem=turn_recv.at[part],
            device_id={"chan": group},
            device_id_type=MESH,
        ).start()

    def all_sent(part):
        return pltpu.make_async_remote_copy(
            src_ref=sent.at[part, pl.ds(0, SHARDS - 1)],
            dst_ref=landed.at[part, pl.ds(0, SHARDS - 1)],
            send_sem=turn_send.at[part],
            recv_sem=turn_recv.at[part],
            device_id={"chan": lax.rem(me + 1, SHARDS)},
            device_id_type=MESH,
        )

    chips = [lax.rem(my_z + away, SHARDS // 2) for away in (4, 3, 5, 2, 6, 1, 7, 0)]

    def leave(part, i):
        if i < len(chips) - 1:
            for core in range(2):
                send(part, chips[i] * 2 + core)
        else:
            send(part, my_z * 2 + 1 - me % 2)

    def build_table(i):
        to_z, table = chips[i], tables[i]
        bins = jnp.broadcast_to(chan_select[pl.ds(to_z, 1), :], (8, LANES))
        other = pltpu.roll(bins, GROUP, 1)
        low = lax.broadcasted_iota(jnp.int32, (8, LANES), 1) < GROUP
        bins = jnp.concatenate([jnp.where(low, bins, other), jnp.where(low, other, bins)], 1)
        quarter = jnp.where(low, 0, FFT // 4)
        quarter = jnp.concatenate([quarter, quarter], 1)
        row = lax.broadcasted_iota(jnp.int32, (8, 2 * LANES), 0)
        cos_p, sin_p = cos_sin(row * 256 * bins % FFT)
        middle = [cos_sin((row + 8 * k) * 16 * bins % FFT) for k in range(MIDDLE // 8)]
        fine = [cos_sin(((row + 8 * k) * bins + quarter) % FFT) for k in range(FINE // 8)]
        cos_v = jnp.concatenate([both[0] for both in fine], 0)
        sin_v = jnp.concatenate([both[1] for both in fine], 0)
        for u in range(MIDDLE):
            cos_u, sin_u = (t[u % 8 : u % 8 + 1] for t in middle[u // 8])
            fine_cos[pl.ds(u * FINE, FINE), :] = cos_u * cos_v - sin_u * sin_v
            fine_sin[pl.ds(u * FINE, FINE), :] = sin_u * cos_v + cos_u * sin_v
        for p in range(COARSE):
            place = pl.ds(p * 256, 256)
            turned_on = cos_p[p : p + 1] * fine_cos[...] - sin_p[p : p + 1] * fine_sin[...]
            table[place, :] = turned_on.astype(BF16)

    def transform(early, i):
        to_z = chips[i]
        spectra = jnp.dot(filt[pl.ds(early * 2 * HEIGHT, 2 * HEIGHT), :], tables[i][...], preferred_element_type=F32)
        spectra = spectra.astype(BF16)
        for core in range(2):
            for half in range(2):
                sent[2 * early + half, to_z * 2 + core] = spectra[
                    half * HEIGHT : (half + 1) * HEIGHT, core * LANES : (core + 1) * LANES
                ]

    build_table(0)
    for i in range(len(chips)):
        if i + 1 < len(chips):
            build_table(i + 1)
        transform(0, i)
        leave(0, i)

    halo = pltpu.make_async_remote_copy(
        src_ref=samples.at[:, pl.ds((FRAMES - TAPS + 1) * FFT, HALO)],
        dst_ref=history,
        send_sem=halo_sems.at[0],
        recv_sem=halo_sems.at[1],
        device_id={"chan": lax.rem(me + 1, SHARDS)},
        device_id_type=MESH,
    )
    halo.start()
    for i in range(len(chips)):
        leave(1, i)

    def early_frames():
        halo.wait_send()
        halo.wait_recv()

        @pl.when(me == 0)
        def _():
            history[...] = jnp.zeros((INPUTS, HALO), BF16)

        filter_frames(1)
        for i in range(len(chips)):
            transform(1, i)
            leave(2, i)
        for i in range(len(chips)):
            leave(3, i)

    def turn_part(part):
        landed[part, me] = sent[part, me]
        all_sent(part).wait_recv()

        def widen(i, carry):
            place = pl.ds(pl.multiple_of(i * 4 * HEIGHT, 4 * HEIGHT), 4 * HEIGHT)
            spread[place, :] = landed[part, pl.ds(i * 4, 4)].astype(F32).reshape(4 * HEIGHT, LANES)
            return carry

        lax.fori_loop(0, SHARDS // 4, widen, 0)
        low = lax.broadcasted_iota(jnp.int32, (GROUP, 2 * DEPTH), 1) < DEPTH

        def turn(k, carry):
            for j in range(2):
                a = 4 * k + 2 * j
                both = jnp.concatenate([spread[pl.ds(a + b, DEPTH, stride=PART), :] for b in range(2)], 0).T
                real, imag = both[:GROUP], both[GROUP:]
                turned[pl.ds(a, GROUP, stride=PART), :] = jnp.where(low, real, pltpu.roll(imag, DEPTH, 1))
                turned[pl.ds(a + 1, GROUP, stride=PART), :] = jnp.where(low, pltpu.roll(real, DEPTH, 1), imag)
            return carry

        lax.fori_loop(0, PART // 4, turn, 0)

        def narrow(c, carry):
            place = pl.ds(pl.multiple_of(c * 16 * PART, 16 * PART), 16 * PART)
            own[part, pl.ds(c * 16, 16)] = turned[place, :].astype(BF16).reshape(16, PART, 2 * DEPTH)
            return carry

        lax.fori_loop(0, GROUP // 16, narrow, 0)

    def copy(kind, part, source, target, partner):
        return pltpu.make_async_remote_copy(
            src_ref=source, dst_ref=target, send_sem=send_sems.at[kind], recv_sem=recv_sems.at[kind, part],
            device_id=partner, device_id_type=MESH,
        )

    def arrived(kind, part):
        copy(kind, part, own.at[part], columns.at[blk, part], to_pair).wait_recv()

    def pass_on(kind, part, slot, start, stop, partner):
        place = columns.at[slot, part, pl.ds(start, stop - start)]
        copy(kind, part, place, place, partner).start()

    def pass_last(part, slot, start, stop, partner):
        place = columns.at[slot, part, pl.ds(start, stop - start)]
        copy(PAIR_FAR, 0, place, place, partner).start()

    def first(part):
        copy(PAIR, part, own.at[part], columns.at[blk, part], to_pair).start()
        copy(UP, part, own.at[part], columns.at[blk, part], to_above).start()
        copy(DOWN, part, own.at[part], columns.at[blk, part], to_below).start()

    def second(part):
        arrived(UP, part)
        pass_on(FAR, part, below, 0, GROUP // 2, to_above)
        pass_on(PAIR_UP, part, below, SPLIT, GROUP, to_pair)
        arrived(DOWN, part)
        pass_on(FAR, part, above, GROUP // 2, GROUP, to_below)
        pass_on(PAIR_DOWN, part, above, SPLIT, GROUP, to_pair)
        arrived(PAIR, part)
        pass_on(PAIR_UP, part, pair, 0, SPLIT, to_above)
        pass_on(PAIR_DOWN, part, pair, 0, SPLIT, to_below)
        copy(ROW, 0, columns.at[pair, part], rows.at[grid, part], to_across).start()

    def third(part):
        arrived(FAR, part)
        pass_last(part, far, SPLIT, GROUP, to_pair)
        arrived(PAIR_UP, part)
        pass_last(part, pair_below, 0, SPLIT // 2, to_above)
        arrived(PAIR_DOWN, part)
        pass_last(part, pair_above, SPLIT // 2, SPLIT, to_below)

    turn_part(0)
    first(0)
    early_frames()
    turn_part(1)
    first(1)
    second(0)
    turn_part(2)
    first(2)
    second(1)
    third(0)
    turn_part(3)
    first(3)
    keeps = [
        pltpu.make_async_copy(own, columns.at[blk], keep_sems.at[0]),
        pltpu.make_async_copy(own, rows.at[grid], keep_sems.at[1]),
    ]
    for local in keeps:
        local.start()
    second(2)
    third(1)
    second(3)
    third(2)
    third(3)
    for local in keeps:
        local.wait()

    def whole(kind):
        return copy(kind, 0, own, columns.at[blk], to_pair)

    whole(PAIR_FAR).wait_recv()
    whole(ROW).wait_recv()
    for kind in range(8):
        whole(kind).wait_send()
    for part in range(PARTS):
        all_sent(part).wait_send()


def gathered_spectra(samples, taps, chan_select):
    vmem = pl.BlockSpec(memory_space=pltpu.VMEM)
    anywhere = pl.BlockSpec(memory_space=pl.ANY)
    return pl.pallas_call(
        spectra_kernel,
        out_shape=[
            jax.ShapeDtypeStruct((8,) + BLOCK, BF16),
            jax.ShapeDtypeStruct((2,) + BLOCK, BF16),
        ],
        in_specs=[vmem, vmem, vmem],
        out_specs=[anywhere, anywhere],
        scratch_shapes=[
            pltpu.VMEM((INPUTS, HALO), BF16),
            pltpu.VMEM((PARTS * HEIGHT, FFT), BF16),
            pltpu.VMEM((256, 2 * LANES), F32),
            pltpu.VMEM((256, 2 * LANES), F32),
            pltpu.VMEM((PARTS, SHARDS, HEIGHT, LANES), BF16),
            pltpu.VMEM((PARTS, SHARDS, HEIGHT, LANES), BF16),
            pltpu.VMEM((SHARDS * HEIGHT, LANES), F32),
            pltpu.VMEM((GROUP * PART, 2 * DEPTH), F32),
            pltpu.VMEM(BLOCK, BF16),
            pltpu.SemaphoreType.DMA((2,)),
            pltpu.SemaphoreType.DMA((PARTS,)),
            pltpu.SemaphoreType.DMA((PARTS,)),
            pltpu.SemaphoreType.DMA((2,)),
            pltpu.SemaphoreType.DMA((8,)),
            pltpu.SemaphoreType.DMA((8, PARTS)),
        ]
        + [pltpu.VMEM((FFT, 2 * LANES), BF16)] * (SHARDS // 2),
        compiler_params=pltpu.CompilerParams(
            collective_id=0, has_side_effects=True, vmem_limit_bytes=VMEM_LIMIT
        ),
        name="spectra",
    )(samples, taps, chan_select)


CHANNELS = 8
CHUNKS = GROUP // CHANNELS


def cross_kernel(rows, columns, out, products, out_sems):
    sign = jnp.where(lax.broadcasted_iota(jnp.int32, (2 * INPUTS, 2 * DEPTH), 1) < DEPTH, 1.0, -1.0).astype(BF16)

    def store(i):
        channels = pl.ds(i * CHANNELS, CHANNELS)
        return pltpu.make_async_copy(products.at[:, channels], out.at[:, channels], out_sems.at[i])

    def operand(data, c):
        early_and_late = []
        for early in range(2):
            halves = [data[:, 2 * early + half, c] for half in range(2)]
            early_and_late.append(jnp.stack(halves, 1).reshape(-1, 2 * DEPTH))
        return early_and_late

    for i in range(CHUNKS):
        for c in range(i * CHANNELS, (i + 1) * CHANNELS):
            left = operand(rows, c)
            quarter = [jnp.concatenate([block[:, DEPTH:], block[:, :DEPTH]], 1) * sign for block in left]
            left = jnp.concatenate([jnp.concatenate(left, 1), jnp.concatenate(quarter, 1)], 0)
            product = lax.dot_general(
                left, jnp.concatenate(operand(columns, c), 1), (((1,), (1,)), ((), ())),
                preferred_element_type=F32,
            ) * (1.0 / SPECTRA)
            products[:, c] = product.reshape(2, 2, INPUTS, 8 * INPUTS)
        store(i).start()
    for i in range(CHUNKS):
        store(i).wait()


def cross_products(rows, columns):
    shape = (2, GROUP, 2, INPUTS, 8 * INPUTS)
    return pl.pallas_call(
        cross_kernel,
        out_shape=jax.ShapeDtypeStruct(shape, F32),
        in_specs=[pl.BlockSpec(memory_space=pltpu.VMEM)] * 2,
        out_specs=pl.BlockSpec(memory_space=pltpu.HBM),
        scratch_shapes=[pltpu.VMEM(shape, F32), pltpu.SemaphoreType.DMA((CHUNKS,))],
        compiler_params=pltpu.CompilerParams(vmem_limit_bytes=CROSS_LIMIT),
        name="cross",
    )(rows, columns)


def body(samples, pfb_taps, chan_select):
    columns, rows = gathered_spectra(samples[0], pfb_taps, chan_select.reshape(SHARDS // 2, LANES))
    return cross_products(rows, columns)


def solution(mesh):
    return jax.shard_map(
        body,
        mesh=mesh,
        in_specs=(P("grid", "blk", "chan"), P(), P()),
        out_specs=P(None, "chan", None, "blk", "grid"),
        check_vma=False,
    )
```

```python
import math

import jax
import jax.numpy as jnp
from jax import lax
from jax.experimental import pallas as pl
from jax.experimental.pallas import tpu as pltpu
from jax.sharding import PartitionSpec as P

MESH = pl.DeviceIdType.MESH
BF16 = jnp.bfloat16
F32 = jnp.float32
VMEM_LIMIT = 22 * 1024 * 1024
CROSS_LIMIT = 24 * 1024 * 1024

FFT = 2048
TAPS = 4
INPUTS = 32
FRAMES = 8
GROUP = 64
SHARDS = 16
SPECTRA = SHARDS * FRAMES
LANES = 2 * GROUP
HALO = (TAPS - 1) * FFT
COARSE, MIDDLE, FINE = 8, 16, 16

PARTS = 4
STEPS = FRAMES // 2
PART = INPUTS // 2
HEIGHT = STEPS * PART
DEPTH = SHARDS * STEPS
BLOCK = (PARTS, GROUP, PART, 2 * DEPTH)
SPLIT = 36
PAIR, UP, DOWN, FAR, PAIR_UP, PAIR_DOWN, PAIR_FAR, ROW = range(8)


def cos_sin(phase):
    turns = (phase + FFT // 8) // (FFT // 4)
    angle = (phase - turns * (FFT // 4)).astype(F32) * (2.0 * math.pi / FFT)
    square = angle * angle
    cosine = 1.0 + square * (-1.0 / 2 + square * (1.0 / 24 + square * (-1.0 / 720 + square * (1.0 / 40320))))
    sine = angle * (1.0 + square * (-1.0 / 6 + square * (1.0 / 120 + square * (-1.0 / 5040 + square * (1.0 / 362880)))))
    odd = turns % 2 == 1
    out_cos = jnp.where(odd, sine, cosine)
    out_sin = jnp.where(odd, cosine, sine)
    return (
        jnp.where((turns == 1) | (turns == 2), -out_cos, out_cos),
        jnp.where((turns == 2) | (turns == 3), -out_sin, out_sin),
    )


def spectra_kernel(
    samples, taps, chan_select, columns, rows, history, filt, fine_cos, fine_sin, sent, landed,
    spread, turned, own, halo_sems, turn_send, turn_recv, keep_sems, send_sems, recv_sems, *tables,
):
    me = lax.axis_index("chan")
    blk = lax.axis_index("blk")
    grid = lax.axis_index("grid")
    my_z = me // 2
    y, x = blk // 2, blk % 2

    def at(y_to, x_to):
        return lax.rem(y_to, 4) * 2 + x_to

    pair = at(y, 1 - x)
    below, above, far = at(y + 3, x), at(y + 1, x), at(y + 2, x)
    pair_below, pair_above = at(y + 3, 1 - x), at(y + 1, 1 - x)
    to_pair, to_below, to_above = {"blk": pair}, {"blk": below}, {"blk": above}
    to_across = {"blk": pair, "grid": 1 - grid}

    barrier = pltpu.get_barrier_semaphore()

    def greet(offset, carry):
        pl.semaphore_signal(barrier, inc=1, device_id={"chan": lax.rem(me + offset, SHARDS)}, device_id_type=MESH)
        return carry

    lax.fori_loop(1, SHARDS, greet, 0)
    for partner in (to_pair, to_below, to_above, to_across):
        pl.semaphore_signal(barrier, inc=1, device_id=partner, device_id_type=MESH)

    width = 512

    def filter_frames(early):
        for step in range(STEPS):
            s = step + STEPS * (1 - early)

            def part(i, carry):
                lanes = pl.multiple_of(i * width, width)
                total = jnp.zeros((INPUTS, width), F32)
                for t in range(TAPS):
                    weight = taps[pl.ds(t, 1), pl.ds(lanes, width)].astype(F32)
                    frame = s + t - (TAPS - 1)
                    if frame < 0:
                        source = history[:, pl.ds((s + t) * FFT + lanes, width)]
                    else:
                        source = samples[:, pl.ds(frame * FFT + lanes, width)]
                    total = total + weight * source.astype(F32)
                total = total.astype(BF16)
                for half in range(2):
                    place = pl.ds(((2 * early + half) * STEPS + step) * PART, PART)
                    filt[place, pl.ds(lanes, width)] = total[half * PART : (half + 1) * PART]
                return carry

            lax.fori_loop(0, FFT // width, part, 0)

    filter_frames(0)
    pl.semaphore_wait(barrier, SHARDS - 1 + 4)

    def send(part, group):
        pltpu.make_async_remote_copy(
            src_ref=sent.at[part, group],
            dst_ref=landed.at[part, me],
            send_sem=turn_send.at[part],
            recv_sem=turn_recv.at[part],
            device_id={"chan": group},
            device_id_type=MESH,
        ).start()

    def all_sent(part):
        return pltpu.make_async_remote_copy(
            src_ref=sent.at[part, pl.ds(0, SHARDS - 1)],
            dst_ref=landed.at[part, pl.ds(0, SHARDS - 1)],
            send_sem=turn_send.at[part],
            recv_sem=turn_recv.at[part],
            device_id={"chan": lax.rem(me + 1, SHARDS)},
            device_id_type=MESH,
        )

    chips = [lax.rem(my_z + away, SHARDS // 2) for away in (4, 3, 5, 2, 6, 1, 7, 0)]

    def leave(part, i):
        if i < len(chips) - 1:
            for core in range(2):
                send(part, chips[i] * 2 + core)
        else:
            send(part, my_z * 2 + 1 - me % 2)

    def build_table(i):
        to_z, table = chips[i], tables[i]
        bins = jnp.broadcast_to(chan_select[pl.ds(to_z, 1), :], (8, LANES))
        other = pltpu.roll(bins, GROUP, 1)
        low = lax.broadcasted_iota(jnp.int32, (8, LANES), 1) < GROUP
        bins = jnp.concatenate([jnp.where(low, bins, other), jnp.where(low, other, bins)], 1)
        quarter = jnp.where(low, 0, FFT // 4)
        quarter = jnp.concatenate([quarter, quarter], 1)
        row = lax.broadcasted_iota(jnp.int32, (8, 2 * LANES), 0)
        cos_p, sin_p = cos_sin(row * 256 * bins % FFT)
        middle = [cos_sin((row + 8 * k) * 16 * bins % FFT) for k in range(MIDDLE // 8)]
        fine = [cos_sin(((row + 8 * k) * bins + quarter) % FFT) for k in range(FINE // 8)]
        cos_v = jnp.concatenate([both[0] for both in fine], 0)
        sin_v = jnp.concatenate([both[1] for both in fine], 0)
        for u in range(MIDDLE):
            cos_u, sin_u = (t[u % 8 : u % 8 + 1] for t in middle[u // 8])
            fine_cos[pl.ds(u * FINE, FINE), :] = cos_u * cos_v - sin_u * sin_v
            fine_sin[pl.ds(u * FINE, FINE), :] = sin_u * cos_v + cos_u * sin_v
        for p in range(COARSE):
            place = pl.ds(p * 256, 256)
            turned_on = cos_p[p : p + 1] * fine_cos[...] - sin_p[p : p + 1] * fine_sin[...]
            table[place, :] = turned_on.astype(BF16)

    def transform(early, i):
        to_z = chips[i]
        spectra = jnp.dot(filt[pl.ds(early * 2 * HEIGHT, 2 * HEIGHT), :], tables[i][...], preferred_element_type=F32)
        spectra = spectra.astype(BF16)
        for core in range(2):
            for half in range(2):
                sent[2 * early + half, to_z * 2 + core] = spectra[
                    half * HEIGHT : (half + 1) * HEIGHT, core * LANES : (core + 1) * LANES
                ]

    build_table(0)
    for i in range(len(chips)):
        if i + 1 < len(chips):
            build_table(i + 1)
        transform(0, i)
        leave(0, i)

    halo = pltpu.make_async_remote_copy(
        src_ref=samples.at[:, pl.ds((FRAMES - TAPS + 1) * FFT, HALO)],
        dst_ref=history,
        send_sem=halo_sems.at[0],
        recv_sem=halo_sems.at[1],
        device_id={"chan": lax.rem(me + 1, SHARDS)},
        device_id_type=MESH,
    )
    for i in range(len(chips)):
        leave(1, i)
    halo.start()

    def early_frames():
        halo.wait_send()
        halo.wait_recv()

        @pl.when(me == 0)
        def _():
            history[...] = jnp.zeros((INPUTS, HALO), BF16)

        filter_frames(1)
        for i in range(len(chips)):
            transform(1, i)
            leave(2, i)
        for i in range(len(chips)):
            leave(3, i)

    def turn_part(part):
        landed[part, me] = sent[part, me]
        all_sent(part).wait_recv()

        def widen(i, carry):
            place = pl.ds(pl.multiple_of(i * 4 * HEIGHT, 4 * HEIGHT), 4 * HEIGHT)
            spread[place, :] = landed[part, pl.ds(i * 4, 4)].astype(F32).reshape(4 * HEIGHT, LANES)
            return carry

        lax.fori_loop(0, SHARDS // 4, widen, 0)
        low = lax.broadcasted_iota(jnp.int32, (GROUP, 2 * DEPTH), 1) < DEPTH

        def turn(k, carry):
            for j in range(2):
                a = 4 * k + 2 * j
                both = jnp.concatenate([spread[pl.ds(a + b, DEPTH, stride=PART), :] for b in range(2)], 0).T
                real, imag = both[:GROUP], both[GROUP:]
                turned[pl.ds(a, GROUP, stride=PART), :] = jnp.where(low, real, pltpu.roll(imag, DEPTH, 1))
                turned[pl.ds(a + 1, GROUP, stride=PART), :] = jnp.where(low, pltpu.roll(real, DEPTH, 1), imag)
            return carry

        lax.fori_loop(0, PART // 4, turn, 0)

        def narrow(c, carry):
            place = pl.ds(pl.multiple_of(c * 16 * PART, 16 * PART), 16 * PART)
            own[part, pl.ds(c * 16, 16)] = turned[place, :].astype(BF16).reshape(16, PART, 2 * DEPTH)
            return carry

        lax.fori_loop(0, GROUP // 16, narrow, 0)

    def copy(kind, part, source, target, partner):
        return pltpu.make_async_remote_copy(
            src_ref=source, dst_ref=target, send_sem=send_sems.at[kind], recv_sem=recv_sems.at[kind, part],
            device_id=partner, device_id_type=MESH,
        )

    def arrived(kind, part):
        copy(kind, part, own.at[part], columns.at[blk, part], to_pair).wait_recv()

    def pass_on(kind, part, slot, start, stop, partner):
        place = columns.at[slot, part, pl.ds(start, stop - start)]
        copy(kind, part, place, place, partner).start()

    def pass_last(part, slot, start, stop, partner):
        place = columns.at[slot, part, pl.ds(start, stop - start)]
        copy(PAIR_FAR, 0, place, place, partner).start()

    def first(part):
        copy(PAIR, part, own.at[part], columns.at[blk, part], to_pair).start()
        copy(UP, part, own.at[part], columns.at[blk, part], to_above).start()
        copy(DOWN, part, own.at[part], columns.at[blk, part], to_below).start()

    def second(part):
        arrived(UP, part)
        pass_on(FAR, part, below, 0, GROUP // 2, to_above)
        pass_on(PAIR_UP, part, below, SPLIT, GROUP, to_pair)
        arrived(DOWN, part)
        pass_on(FAR, part, above, GROUP // 2, GROUP, to_below)
        pass_on(PAIR_DOWN, part, above, SPLIT, GROUP, to_pair)
        arrived(PAIR, part)
        pass_on(PAIR_UP, part, pair, 0, SPLIT, to_above)
        pass_on(PAIR_DOWN, part, pair, 0, SPLIT, to_below)
        copy(ROW, 0, columns.at[pair, part], rows.at[grid, part], to_across).start()

    def third(part):
        arrived(FAR, part)
        pass_last(part, far, SPLIT, GROUP, to_pair)
        arrived(PAIR_UP, part)
        pass_last(part, pair_below, 0, SPLIT // 2, to_above)
        arrived(PAIR_DOWN, part)
        pass_last(part, pair_above, SPLIT // 2, SPLIT, to_below)

    turn_part(0)
    first(0)
    turn_part(1)
    first(1)
    second(0)
    early_frames()
    second(1)
    turn_part(2)
    first(2)
    third(0)
    turn_part(3)
    first(3)
    keeps = [
        pltpu.make_async_copy(own, columns.at[blk], keep_sems.at[0]),
        pltpu.make_async_copy(own, rows.at[grid], keep_sems.at[1]),
    ]
    for local in keeps:
        local.start()
    third(1)
    second(2)
    second(3)
    third(2)
    third(3)
    for local in keeps:
        local.wait()

    def whole(kind):
        return copy(kind, 0, own, columns.at[blk], to_pair)

    whole(PAIR_FAR).wait_recv()
    whole(ROW).wait_recv()
    for kind in range(8):
        whole(kind).wait_send()
    for part in range(PARTS):
        all_sent(part).wait_send()


def gathered_spectra(samples, taps, chan_select):
    vmem = pl.BlockSpec(memory_space=pltpu.VMEM)
    anywhere = pl.BlockSpec(memory_space=pl.ANY)
    return pl.pallas_call(
        spectra_kernel,
        out_shape=[
            jax.ShapeDtypeStruct((8,) + BLOCK, BF16),
            jax.ShapeDtypeStruct((2,) + BLOCK, BF16),
        ],
        in_specs=[vmem, vmem, vmem],
        out_specs=[anywhere, anywhere],
        scratch_shapes=[
            pltpu.VMEM((INPUTS, HALO), BF16),
            pltpu.VMEM((PARTS * HEIGHT, FFT), BF16),
            pltpu.VMEM((256, 2 * LANES), F32),
            pltpu.VMEM((256, 2 * LANES), F32),
            pltpu.VMEM((PARTS, SHARDS, HEIGHT, LANES), BF16),
            pltpu.VMEM((PARTS, SHARDS, HEIGHT, LANES), BF16),
            pltpu.VMEM((SHARDS * HEIGHT, LANES), F32),
            pltpu.VMEM((GROUP * PART, 2 * DEPTH), F32),
            pltpu.VMEM(BLOCK, BF16),
            pltpu.SemaphoreType.DMA((2,)),
            pltpu.SemaphoreType.DMA((PARTS,)),
            pltpu.SemaphoreType.DMA((PARTS,)),
            pltpu.SemaphoreType.DMA((2,)),
            pltpu.SemaphoreType.DMA((8,)),
            pltpu.SemaphoreType.DMA((8, PARTS)),
        ]
        + [pltpu.VMEM((FFT, 2 * LANES), BF16)] * (SHARDS // 2),
        compiler_params=pltpu.CompilerParams(
            collective_id=0, has_side_effects=True, vmem_limit_bytes=VMEM_LIMIT
        ),
        name="spectra",
    )(samples, taps, chan_select)


CHANNELS = 8
CHUNKS = GROUP // CHANNELS


def cross_kernel(rows, columns, out, products, out_sems):
    sign = jnp.where(lax.broadcasted_iota(jnp.int32, (2 * INPUTS, 2 * DEPTH), 1) < DEPTH, 1.0, -1.0).astype(BF16)

    def store(i):
        channels = pl.ds(i * CHANNELS, CHANNELS)
        return pltpu.make_async_copy(products.at[:, channels], out.at[:, channels], out_sems.at[i])

    def operand(data, c):
        early_and_late = []
        for early in range(2):
            halves = [data[:, 2 * early + half, c] for half in range(2)]
            early_and_late.append(jnp.stack(halves, 1).reshape(-1, 2 * DEPTH))
        return early_and_late

    for i in range(CHUNKS):
        for c in range(i * CHANNELS, (i + 1) * CHANNELS):
            left = operand(rows, c)
            quarter = [jnp.concatenate([block[:, DEPTH:], block[:, :DEPTH]], 1) * sign for block in left]
            left = jnp.concatenate([jnp.concatenate(left, 1), jnp.concatenate(quarter, 1)], 0)
            product = lax.dot_general(
                left, jnp.concatenate(operand(columns, c), 1), (((1,), (1,)), ((), ())),
                preferred_element_type=F32,
            ) * (1.0 / SPECTRA)
            products[:, c] = product.reshape(2, 2, INPUTS, 8 * INPUTS)
        store(i).start()
    for i in range(CHUNKS):
        store(i).wait()


def cross_products(rows, columns):
    shape = (2, GROUP, 2, INPUTS, 8 * INPUTS)
    return pl.pallas_call(
        cross_kernel,
        out_shape=jax.ShapeDtypeStruct(shape, F32),
        in_specs=[pl.BlockSpec(memory_space=pltpu.VMEM)] * 2,
        out_specs=pl.BlockSpec(memory_space=pltpu.HBM),
        scratch_shapes=[pltpu.VMEM(shape, F32), pltpu.SemaphoreType.DMA((CHUNKS,))],
        compiler_params=pltpu.CompilerParams(vmem_limit_bytes=CROSS_LIMIT),
        name="cross",
    )(rows, columns)


def body(samples, pfb_taps, chan_select):
    columns, rows = gathered_spectra(samples[0], pfb_taps, chan_select.reshape(SHARDS // 2, LANES))
    return cross_products(rows, columns)


def solution(mesh):
    return jax.shard_map(
        body,
        mesh=mesh,
        in_specs=(P("grid", "blk", "chan"), P(), P()),
        out_specs=P(None, "chan", None, "blk", "grid"),
        check_vma=False,
    )
```

```python
import math

import jax
import jax.numpy as jnp
from jax import lax
from jax.experimental import pallas as pl
from jax.experimental.pallas import tpu as pltpu
from jax.sharding import PartitionSpec as P

MESH = pl.DeviceIdType.MESH
BF16 = jnp.bfloat16
F32 = jnp.float32
VMEM_LIMIT = 22 * 1024 * 1024
CROSS_LIMIT = 24 * 1024 * 1024

FFT = 2048
TAPS = 4
INPUTS = 32
FRAMES = 8
GROUP = 64
SHARDS = 16
SPECTRA = SHARDS * FRAMES
LANES = 2 * GROUP
HALO = (TAPS - 1) * FFT
COARSE, MIDDLE, FINE = 8, 16, 16

PARTS = 4
STEPS = FRAMES // 2
PART = INPUTS // 2
HEIGHT = STEPS * PART
DEPTH = SHARDS * STEPS
BLOCK = (PARTS, GROUP, PART, 2 * DEPTH)
SPLIT = 35
PAIR, UP, DOWN, FAR, PAIR_UP, PAIR_DOWN, PAIR_FAR, ROW = range(8)


def cos_sin(phase):
    turns = (phase + FFT // 8) // (FFT // 4)
    angle = (phase - turns * (FFT // 4)).astype(F32) * (2.0 * math.pi / FFT)
    square = angle * angle
    cosine = 1.0 + square * (-1.0 / 2 + square * (1.0 / 24 + square * (-1.0 / 720 + square * (1.0 / 40320))))
    sine = angle * (1.0 + square * (-1.0 / 6 + square * (1.0 / 120 + square * (-1.0 / 5040 + square * (1.0 / 362880)))))
    odd = turns % 2 == 1
    out_cos = jnp.where(odd, sine, cosine)
    out_sin = jnp.where(odd, cosine, sine)
    return (
        jnp.where((turns == 1) | (turns == 2), -out_cos, out_cos),
        jnp.where((turns == 2) | (turns == 3), -out_sin, out_sin),
    )


def spectra_kernel(
    samples, taps, chan_select, columns, rows, history, filt, sent, landed,
    spread, turned, own, halo_sems, turn_send, turn_recv, keep_sems, send_sems, recv_sems, *tables,
):
    me = lax.axis_index("chan")
    blk = lax.axis_index("blk")
    grid = lax.axis_index("grid")
    my_z = me // 2
    y, x = blk // 2, blk % 2

    def at(y_to, x_to):
        return lax.rem(y_to, 4) * 2 + x_to

    pair = at(y, 1 - x)
    below, above, far = at(y + 3, x), at(y + 1, x), at(y + 2, x)
    pair_below, pair_above = at(y + 3, 1 - x), at(y + 1, 1 - x)
    to_pair, to_below, to_above = {"blk": pair}, {"blk": below}, {"blk": above}
    to_across = {"blk": pair, "grid": 1 - grid}

    barrier = pltpu.get_barrier_semaphore()

    def greet(offset, carry):
        pl.semaphore_signal(barrier, inc=1, device_id={"chan": lax.rem(me + offset, SHARDS)}, device_id_type=MESH)
        return carry

    lax.fori_loop(1, SHARDS, greet, 0)
    for partner in (to_pair, to_below, to_above, to_across):
        pl.semaphore_signal(barrier, inc=1, device_id=partner, device_id_type=MESH)

    width = 512

    def filter_frames(early):
        for step in range(STEPS):
            s = step + STEPS * (1 - early)

            def part(i, carry):
                lanes = pl.multiple_of(i * width, width)
                total = jnp.zeros((INPUTS, width), F32)
                for t in range(TAPS):
                    weight = taps[pl.ds(t, 1), pl.ds(lanes, width)].astype(F32)
                    frame = s + t - (TAPS - 1)
                    if frame < 0:
                        source = history[:, pl.ds((s + t) * FFT + lanes, width)]
                    else:
                        source = samples[:, pl.ds(frame * FFT + lanes, width)]
                    total = total + weight * source.astype(F32)
                total = total.astype(BF16)
                for half in range(2):
                    place = pl.ds(((2 * early + half) * STEPS + step) * PART, PART)
                    filt[place, pl.ds(lanes, width)] = total[half * PART : (half + 1) * PART]
                return carry

            lax.fori_loop(0, FFT // width, part, 0)

    filter_frames(0)
    pl.semaphore_wait(barrier, SHARDS - 1 + 4)

    def send(part, group):
        pltpu.make_async_remote_copy(
            src_ref=sent.at[part, group],
            dst_ref=landed.at[part, me],
            send_sem=turn_send.at[part],
            recv_sem=turn_recv.at[part],
            device_id={"chan": group},
            device_id_type=MESH,
        ).start()

    def all_sent(part):
        return pltpu.make_async_remote_copy(
            src_ref=sent.at[part, pl.ds(0, SHARDS - 1)],
            dst_ref=landed.at[part, pl.ds(0, SHARDS - 1)],
            send_sem=turn_send.at[part],
            recv_sem=turn_recv.at[part],
            device_id={"chan": lax.rem(me + 1, SHARDS)},
            device_id_type=MESH,
        )

    chips = [lax.rem(my_z + away, SHARDS // 2) for away in (4, 3, 5, 2, 6, 1, 7, 0)]

    def leave(part, i):
        if i < len(chips) - 1:
            for core in range(2):
                send(part, chips[i] * 2 + core)
        else:
            send(part, my_z * 2 + 1 - me % 2)

    def build_table(i):
        to_z, table = chips[i], tables[i]
        bins = jnp.broadcast_to(chan_select[pl.ds(to_z, 1), :], (8, LANES))
        other = pltpu.roll(bins, GROUP, 1)
        low = lax.broadcasted_iota(jnp.int32, (8, LANES), 1) < GROUP
        bins = jnp.concatenate([jnp.where(low, bins, other), jnp.where(low, other, bins)], 1)
        quarter = jnp.where(low, 0, FFT // 4)
        quarter = jnp.concatenate([quarter, quarter], 1)
        row = lax.broadcasted_iota(jnp.int32, (8, 2 * LANES), 0)
        cos_p, sin_p = cos_sin(row * 256 * bins % FFT)
        middle = [cos_sin((row + 8 * k) * 16 * bins % FFT) for k in range(MIDDLE // 8)]
        fine = [cos_sin(((row + 8 * k) * bins + quarter) % FFT) for k in range(FINE // 8)]
        cos_v = jnp.concatenate([both[0] for both in fine], 0)
        sin_v = jnp.concatenate([both[1] for both in fine], 0)
        for u in range(MIDDLE):
            cos_u, sin_u = (t[u % 8 : u % 8 + 1] for t in middle[u // 8])
            fine_cos = cos_u * cos_v - sin_u * sin_v
            fine_sin = sin_u * cos_v + cos_u * sin_v
            for p in range(COARSE):
                turned_on = cos_p[p : p + 1] * fine_cos - sin_p[p : p + 1] * fine_sin
                table[pl.ds(p * 256 + u * FINE, FINE), :] = turned_on.astype(BF16)

    def transform(early, i):
        to_z = chips[i]
        spectra = jnp.dot(filt[pl.ds(early * 2 * HEIGHT, 2 * HEIGHT), :], tables[i][...], preferred_element_type=F32)
        spectra = spectra.astype(BF16)
        for core in range(2):
            for half in range(2):
                sent[2 * early + half, to_z * 2 + core] = spectra[
                    half * HEIGHT : (half + 1) * HEIGHT, core * LANES : (core + 1) * LANES
                ]

    build_table(0)
    for i in range(len(chips)):
        if i + 1 < len(chips):
            build_table(i + 1)
        transform(0, i)
        leave(0, i)

    halo = pltpu.make_async_remote_copy(
        src_ref=samples.at[:, pl.ds((FRAMES - TAPS + 1) * FFT, HALO)],
        dst_ref=history,
        send_sem=halo_sems.at[0],
        recv_sem=halo_sems.at[1],
        device_id={"chan": lax.rem(me + 1, SHARDS)},
        device_id_type=MESH,
    )
    for i in range(len(chips)):
        leave(1, i)
    halo.start()

    def early_frames():
        halo.wait_send()
        halo.wait_recv()

        @pl.when(me == 0)
        def _():
            history[...] = jnp.zeros((INPUTS, HALO), BF16)

        filter_frames(1)
        for i in range(len(chips)):
            transform(1, i)
            leave(2, i)
        for i in range(len(chips)):
            leave(3, i)

    def turn_part(part):
        landed[part, me] = sent[part, me]
        all_sent(part).wait_recv()

        def widen(i, carry):
            place = pl.ds(i * 4 * HEIGHT, 4 * HEIGHT)
            spread[place, :] = landed[part, pl.ds(i * 4, 4)].astype(F32).reshape(4 * HEIGHT, LANES)
            return carry

        for k in range(SHARDS // 4):
            widen(k, 0)
        low = lax.broadcasted_iota(jnp.int32, (GROUP, 2 * DEPTH), 1) < DEPTH

        def turn(k, carry):
            for j in range(2):
                a = 4 * k + 2 * j
                both = jnp.concatenate([spread[pl.ds(a + b, DEPTH, stride=PART), :] for b in range(2)], 0).T
                real, imag = both[:GROUP], both[GROUP:]
                turned[pl.ds(a, GROUP, stride=PART), :] = jnp.where(low, real, pltpu.roll(imag, DEPTH, 1))
                turned[pl.ds(a + 1, GROUP, stride=PART), :] = jnp.where(low, pltpu.roll(real, DEPTH, 1), imag)
            return carry

        for k in range(PART // 4):
            turn(k, 0)

        def narrow(c, carry):
            place = pl.ds(c * 16 * PART, 16 * PART)
            own[part, pl.ds(c * 16, 16)] = turned[place, :].astype(BF16).reshape(16, PART, 2 * DEPTH)
            return carry

        for k in range(GROUP // 16):
            narrow(k, 0)

    def copy(kind, part, source, target, partner):
        return pltpu.make_async_remote_copy(
            src_ref=source, dst_ref=target, send_sem=send_sems.at[kind], recv_sem=recv_sems.at[kind, part],
            device_id=partner, device_id_type=MESH,
        )

    def arrived(kind, part):
        copy(kind, part, own.at[part], columns.at[blk, part], to_pair).wait_recv()

    def pass_on(kind, part, slot, start, stop, partner):
        place = columns.at[slot, part, pl.ds(start, stop - start)]
        copy(kind, part, place, place, partner).start()

    def pass_last(part, slot, start, stop, partner):
        place = columns.at[slot, part, pl.ds(start, stop - start)]
        copy(PAIR_FAR, 0, place, place, partner).start()

    def first(part):
        copy(UP, part, own.at[part], columns.at[blk, part], to_above).start()
        copy(DOWN, part, own.at[part], columns.at[blk, part], to_below).start()
        copy(PAIR, part, own.at[part], columns.at[blk, part], to_pair).start()

    def second(part):
        arrived(UP, part)
        pass_on(FAR, part, below, 0, GROUP // 2, to_above)
        pass_on(PAIR_UP, part, below, SPLIT, GROUP, to_pair)
        arrived(DOWN, part)
        pass_on(FAR, part, above, GROUP // 2, GROUP, to_below)
        pass_on(PAIR_DOWN, part, above, SPLIT, GROUP, to_pair)
        arrived(PAIR, part)
        pass_on(PAIR_UP, part, pair, 0, SPLIT, to_above)
        pass_on(PAIR_DOWN, part, pair, 0, SPLIT, to_below)
        copy(ROW, 0, columns.at[pair, part], rows.at[grid, part], to_across).start()

    def third(part):
        arrived(FAR, part)
        pass_last(part, far, SPLIT, GROUP, to_pair)
        arrived(PAIR_UP, part)
        pass_last(part, pair_below, 0, (SPLIT // 2 + 1), to_above)
        arrived(PAIR_DOWN, part)
        pass_last(part, pair_above, (SPLIT // 2 + 1), SPLIT, to_below)

    turn_part(0)
    first(0)
    turn_part(1)
    first(1)
    second(0)
    early_frames()
    second(1)
    turn_part(2)
    first(2)
    third(0)
    turn_part(3)
    first(3)
    keeps = [
        pltpu.make_async_copy(own, columns.at[blk], keep_sems.at[0]),
        pltpu.make_async_copy(own, rows.at[grid], keep_sems.at[1]),
    ]
    for local in keeps:
        local.start()
    third(1)
    second(2)
    second(3)
    third(2)
    third(3)
    for local in keeps:
        local.wait()

    def whole(kind):
        return copy(kind, 0, own, columns.at[blk], to_pair)

    whole(PAIR_FAR).wait_recv()
    whole(ROW).wait_recv()
    for kind in range(8):
        whole(kind).wait_send()
    for part in range(PARTS):
        all_sent(part).wait_send()


def gathered_spectra(samples, taps, chan_select):
    vmem = pl.BlockSpec(memory_space=pltpu.VMEM)
    anywhere = pl.BlockSpec(memory_space=pl.ANY)
    return pl.pallas_call(
        spectra_kernel,
        out_shape=[
            jax.ShapeDtypeStruct((8,) + BLOCK, BF16),
            jax.ShapeDtypeStruct((2,) + BLOCK, BF16),
        ],
        in_specs=[vmem, vmem, vmem],
        out_specs=[anywhere, anywhere],
        scratch_shapes=[
            pltpu.VMEM((INPUTS, HALO), BF16),
            pltpu.VMEM((PARTS * HEIGHT, FFT), BF16),
            pltpu.VMEM((PARTS, SHARDS, HEIGHT, LANES), BF16),
            pltpu.VMEM((PARTS, SHARDS, HEIGHT, LANES), BF16),
            pltpu.VMEM((SHARDS * HEIGHT, LANES), F32),
            pltpu.VMEM((GROUP * PART, 2 * DEPTH), F32),
            pltpu.VMEM(BLOCK, BF16),
            pltpu.SemaphoreType.DMA((2,)),
            pltpu.SemaphoreType.DMA((PARTS,)),
            pltpu.SemaphoreType.DMA((PARTS,)),
            pltpu.SemaphoreType.DMA((2,)),
            pltpu.SemaphoreType.DMA((8,)),
            pltpu.SemaphoreType.DMA((8, PARTS)),
        ]
        + [pltpu.VMEM((FFT, 2 * LANES), BF16)] * (SHARDS // 2),
        compiler_params=pltpu.CompilerParams(
            collective_id=0, has_side_effects=True, vmem_limit_bytes=VMEM_LIMIT
        ),
        name="spectra",
    )(samples, taps, chan_select)


CHANNELS = 8
CHUNKS = GROUP // CHANNELS


def cross_kernel(rows, columns, out, products, out_sems):
    sign = jnp.where(lax.broadcasted_iota(jnp.int32, (2 * INPUTS, 2 * DEPTH), 1) < DEPTH, 1.0, -1.0).astype(BF16)

    def store(i):
        channels = pl.ds(i * CHANNELS, CHANNELS)
        return pltpu.make_async_copy(products.at[:, channels], out.at[:, channels], out_sems.at[i])

    def operand(data, c):
        early_and_late = []
        for early in range(2):
            halves = [data[:, 2 * early + half, c] for half in range(2)]
            early_and_late.append(jnp.stack(halves, 1).reshape(-1, 2 * DEPTH))
        return early_and_late

    for i in range(CHUNKS):
        for c in range(i * CHANNELS, (i + 1) * CHANNELS):
            left = operand(rows, c)
            quarter = [jnp.concatenate([block[:, DEPTH:], block[:, :DEPTH]], 1) * sign for block in left]
            left = jnp.concatenate([jnp.concatenate(left, 1), jnp.concatenate(quarter, 1)], 0)
            product = lax.dot_general(
                left, jnp.concatenate(operand(columns, c), 1), (((1,), (1,)), ((), ())),
                preferred_element_type=F32,
            ) * (1.0 / SPECTRA)
            products[:, c] = product.reshape(2, 2, INPUTS, 8 * INPUTS)
        store(i).start()
    for i in range(CHUNKS):
        store(i).wait()


def cross_products(rows, columns):
    shape = (2, GROUP, 2, INPUTS, 8 * INPUTS)
    return pl.pallas_call(
        cross_kernel,
        out_shape=jax.ShapeDtypeStruct(shape, F32),
        in_specs=[pl.BlockSpec(memory_space=pltpu.VMEM)] * 2,
        out_specs=pl.BlockSpec(memory_space=pltpu.HBM),
        scratch_shapes=[pltpu.VMEM(shape, F32), pltpu.SemaphoreType.DMA((CHUNKS,))],
        compiler_params=pltpu.CompilerParams(vmem_limit_bytes=CROSS_LIMIT),
        name="cross",
    )(rows, columns)


def body(samples, pfb_taps, chan_select):
    columns, rows = gathered_spectra(samples[0], pfb_taps, chan_select.reshape(SHARDS // 2, LANES))
    return cross_products(rows, columns)


def solution(mesh):
    return jax.shard_map(
        body,
        mesh=mesh,
        in_specs=(P("grid", "blk", "chan"), P(), P()),
        out_specs=P(None, "chan", None, "blk", "grid"),
        check_vma=False,
    )
```

```python
import math

import jax
import jax.numpy as jnp
from jax import lax
from jax.experimental import pallas as pl
from jax.experimental.pallas import tpu as pltpu
from jax.sharding import PartitionSpec as P

MESH = pl.DeviceIdType.MESH
BF16 = jnp.bfloat16
F32 = jnp.float32
VMEM_LIMIT = 22 * 1024 * 1024
CROSS_LIMIT = 24 * 1024 * 1024

FFT = 2048
TAPS = 4
INPUTS = 32
FRAMES = 8
GROUP = 64
SHARDS = 16
SPECTRA = SHARDS * FRAMES
LANES = 2 * GROUP
HALO = (TAPS - 1) * FFT
COARSE, MIDDLE, FINE = 8, 16, 16

PARTS = 4
STEPS = FRAMES // 2
PART = INPUTS // 2
HEIGHT = STEPS * PART
DEPTH = SHARDS * STEPS
BLOCK = (PARTS, GROUP, PART, 2 * DEPTH)
SPLIT = 35
PAIR, UP, DOWN, FAR, PAIR_UP, PAIR_DOWN, PAIR_FAR, ROW = range(8)


def cos_sin(phase):
    turns = (phase + FFT // 8) // (FFT // 4)
    angle = (phase - turns * (FFT // 4)).astype(F32) * (2.0 * math.pi / FFT)
    square = angle * angle
    cosine = 1.0 + square * (-1.0 / 2 + square * (1.0 / 24 + square * (-1.0 / 720 + square * (1.0 / 40320))))
    sine = angle * (1.0 + square * (-1.0 / 6 + square * (1.0 / 120 + square * (-1.0 / 5040 + square * (1.0 / 362880)))))
    odd = turns % 2 == 1
    out_cos = jnp.where(odd, sine, cosine)
    out_sin = jnp.where(odd, cosine, sine)
    return (
        jnp.where((turns == 1) | (turns == 2), -out_cos, out_cos),
        jnp.where((turns == 2) | (turns == 3), -out_sin, out_sin),
    )


def spectra_kernel(
    samples, taps, chan_select, columns, rows, history, filt, sent, landed,
    spread, turned, own, halo_sems, turn_send, turn_recv, keep_sems, send_sems, recv_sems, *tables,
):
    me = lax.axis_index("chan")
    blk = lax.axis_index("blk")
    grid = lax.axis_index("grid")
    my_z = me // 2
    y, x = blk // 2, blk % 2

    def at(y_to, x_to):
        return lax.rem(y_to, 4) * 2 + x_to

    pair = at(y, 1 - x)
    below, above, far = at(y + 3, x), at(y + 1, x), at(y + 2, x)
    pair_below, pair_above = at(y + 3, 1 - x), at(y + 1, 1 - x)
    to_pair, to_below, to_above = {"blk": pair}, {"blk": below}, {"blk": above}
    to_across = {"blk": pair, "grid": 1 - grid}

    barrier = pltpu.get_barrier_semaphore()

    def greet(offset, carry):
        pl.semaphore_signal(barrier, inc=1, device_id={"chan": lax.rem(me + offset, SHARDS)}, device_id_type=MESH)
        return carry

    for offset in range(1, SHARDS):
        greet(offset, 0)
    for partner in (to_pair, to_below, to_above, to_across):
        pl.semaphore_signal(barrier, inc=1, device_id=partner, device_id_type=MESH)

    width = 512

    def filter_frames(early):
        for step in range(STEPS):
            s = step + STEPS * (1 - early)

            def part(i, carry):
                lanes = i * width
                total = jnp.zeros((INPUTS, width), F32)
                for t in range(TAPS):
                    weight = taps[pl.ds(t, 1), pl.ds(lanes, width)].astype(F32)
                    frame = s + t - (TAPS - 1)
                    if frame < 0:
                        source = history[:, pl.ds((s + t) * FFT + lanes, width)]
                    else:
                        source = samples[:, pl.ds(frame * FFT + lanes, width)]
                    total = total + weight * source.astype(F32)
                total = total.astype(BF16)
                for half in range(2):
                    place = pl.ds(((2 * early + half) * STEPS + step) * PART, PART)
                    filt[place, pl.ds(lanes, width)] = total[half * PART : (half + 1) * PART]
                return carry

            for i in range(FFT // width):
                part(i, 0)

    filter_frames(0)
    pl.semaphore_wait(barrier, SHARDS - 1 + 4)

    def send(part, group):
        pltpu.make_async_remote_copy(
            src_ref=sent.at[part, group],
            dst_ref=landed.at[part, me],
            send_sem=turn_send.at[part],
            recv_sem=turn_recv.at[part],
            device_id={"chan": group},
            device_id_type=MESH,
        ).start()

    def all_sent(part):
        return pltpu.make_async_remote_copy(
            src_ref=sent.at[part, pl.ds(0, SHARDS - 1)],
            dst_ref=landed.at[part, pl.ds(0, SHARDS - 1)],
            send_sem=turn_send.at[part],
            recv_sem=turn_recv.at[part],
            device_id={"chan": lax.rem(me + 1, SHARDS)},
            device_id_type=MESH,
        )

    chips = [lax.rem(my_z + away, SHARDS // 2) for away in (4, 3, 5, 2, 6, 1, 7, 0)]

    def leave(part, i):
        if i < len(chips) - 1:
            for core in range(2):
                send(part, chips[i] * 2 + core)
        else:
            send(part, my_z * 2 + 1 - me % 2)

    def build_table(i):
        to_z, table = chips[i], tables[i]
        bins = jnp.broadcast_to(chan_select[pl.ds(to_z, 1), :], (8, LANES))
        other = pltpu.roll(bins, GROUP, 1)
        low = lax.broadcasted_iota(jnp.int32, (8, LANES), 1) < GROUP
        bins = jnp.concatenate([jnp.where(low, bins, other), jnp.where(low, other, bins)], 1)
        quarter = jnp.where(low, 0, FFT // 4)
        quarter = jnp.concatenate([quarter, quarter], 1)
        row = lax.broadcasted_iota(jnp.int32, (8, 2 * LANES), 0)
        cos_p, sin_p = cos_sin(row * 256 * bins % FFT)
        middle = [cos_sin((row + 8 * k) * 16 * bins % FFT) for k in range(MIDDLE // 8)]
        fine = [cos_sin(((row + 8 * k) * bins + quarter) % FFT) for k in range(FINE // 8)]
        cos_v = jnp.concatenate([both[0] for both in fine], 0)
        sin_v = jnp.concatenate([both[1] for both in fine], 0)
        for u in range(MIDDLE):
            cos_u, sin_u = (t[u % 8 : u % 8 + 1] for t in middle[u // 8])
            fine_cos = cos_u * cos_v - sin_u * sin_v
            fine_sin = sin_u * cos_v + cos_u * sin_v
            for p in range(COARSE):
                turned_on = cos_p[p : p + 1] * fine_cos - sin_p[p : p + 1] * fine_sin
                table[pl.ds(p * 256 + u * FINE, FINE), :] = turned_on.astype(BF16)

    def transform(early, i):
        to_z = chips[i]
        spectra = jnp.dot(filt[pl.ds(early * 2 * HEIGHT, 2 * HEIGHT), :], tables[i][...], preferred_element_type=F32)
        spectra = spectra.astype(BF16)
        for core in range(2):
            for half in range(2):
                sent[2 * early + half, to_z * 2 + core] = spectra[
                    half * HEIGHT : (half + 1) * HEIGHT, core * LANES : (core + 1) * LANES
                ]

    build_table(0)
    for i in range(len(chips)):
        if i + 1 < len(chips):
            build_table(i + 1)
        transform(0, i)
        leave(0, i)

    halo = pltpu.make_async_remote_copy(
        src_ref=samples.at[:, pl.ds((FRAMES - TAPS + 1) * FFT, HALO)],
        dst_ref=history,
        send_sem=halo_sems.at[0],
        recv_sem=halo_sems.at[1],
        device_id={"chan": lax.rem(me + 1, SHARDS)},
        device_id_type=MESH,
    )
    for i in range(len(chips)):
        leave(1, i)
    halo.start()

    def early_frames():
        halo.wait_send()
        halo.wait_recv()

        @pl.when(me == 0)
        def _():
            history[...] = jnp.zeros((INPUTS, HALO), BF16)

        filter_frames(1)
        for i in range(len(chips)):
            transform(1, i)
            leave(2, i)
        for i in range(len(chips)):
            leave(3, i)

    def turn_part(part):
        landed[part, me] = sent[part, me]
        all_sent(part).wait_recv()

        def widen(i, carry):
            place = pl.ds(i * 4 * HEIGHT, 4 * HEIGHT)
            spread[place, :] = landed[part, pl.ds(i * 4, 4)].astype(F32).reshape(4 * HEIGHT, LANES)
            return carry

        for k in range(SHARDS // 4):
            widen(k, 0)
        low = lax.broadcasted_iota(jnp.int32, (GROUP, 2 * DEPTH), 1) < DEPTH

        def turn(k, carry):
            for j in range(2):
                a = 4 * k + 2 * j
                both = jnp.concatenate([spread[pl.ds(a + b, DEPTH, stride=PART), :] for b in range(2)], 0).T
                real, imag = both[:GROUP], both[GROUP:]
                turned[pl.ds(a, GROUP, stride=PART), :] = jnp.where(low, real, pltpu.roll(imag, DEPTH, 1))
                turned[pl.ds(a + 1, GROUP, stride=PART), :] = jnp.where(low, pltpu.roll(real, DEPTH, 1), imag)
            return carry

        for k in range(PART // 4):
            turn(k, 0)

        def narrow(c, carry):
            place = pl.ds(c * 16 * PART, 16 * PART)
            own[part, pl.ds(c * 16, 16)] = turned[place, :].astype(BF16).reshape(16, PART, 2 * DEPTH)
            return carry

        for k in range(GROUP // 16):
            narrow(k, 0)

    def copy(kind, part, source, target, partner):
        return pltpu.make_async_remote_copy(
            src_ref=source, dst_ref=target, send_sem=send_sems.at[kind], recv_sem=recv_sems.at[kind, part],
            device_id=partner, device_id_type=MESH,
        )

    def arrived(kind, part):
        copy(kind, part, own.at[part], columns.at[blk, part], to_pair).wait_recv()

    def pass_on(kind, part, slot, start, stop, partner):
        place = columns.at[slot, part, pl.ds(start, stop - start)]
        copy(kind, part, place, place, partner).start()

    def pass_last(part, slot, start, stop, partner):
        place = columns.at[slot, part, pl.ds(start, stop - start)]
        copy(PAIR_FAR, 0, place, place, partner).start()

    def first(part):
        copy(UP, part, own.at[part], columns.at[blk, part], to_above).start()
        copy(DOWN, part, own.at[part], columns.at[blk, part], to_below).start()
        copy(PAIR, part, own.at[part], columns.at[blk, part], to_pair).start()

    def second(part):
        arrived(UP, part)
        pass_on(FAR, part, below, 0, GROUP // 2, to_above)
        pass_on(PAIR_UP, part, below, SPLIT, GROUP, to_pair)
        arrived(DOWN, part)
        pass_on(FAR, part, above, GROUP // 2, GROUP, to_below)
        pass_on(PAIR_DOWN, part, above, SPLIT, GROUP, to_pair)
        arrived(PAIR, part)
        pass_on(PAIR_UP, part, pair, 0, SPLIT, to_above)
        pass_on(PAIR_DOWN, part, pair, 0, SPLIT, to_below)
        copy(ROW, 0, columns.at[pair, part], rows.at[grid, part], to_across).start()

    def third(part):
        arrived(FAR, part)
        pass_last(part, far, SPLIT, GROUP, to_pair)
        arrived(PAIR_UP, part)
        pass_last(part, pair_below, 0, (SPLIT // 2 + 1), to_above)
        arrived(PAIR_DOWN, part)
        pass_last(part, pair_above, (SPLIT // 2 + 1), SPLIT, to_below)

    turn_part(0)
    first(0)
    turn_part(1)
    first(1)
    second(0)
    early_frames()
    second(1)
    turn_part(2)
    first(2)
    third(0)
    turn_part(3)
    first(3)
    keeps = [
        pltpu.make_async_copy(own, columns.at[blk], keep_sems.at[0]),
        pltpu.make_async_copy(own, rows.at[grid], keep_sems.at[1]),
    ]
    for local in keeps:
        local.start()
    third(1)
    second(2)
    second(3)
    third(2)
    third(3)
    for local in keeps:
        local.wait()

    def whole(kind):
        return copy(kind, 0, own, columns.at[blk], to_pair)

    whole(PAIR_FAR).wait_recv()
    whole(ROW).wait_recv()
    for kind in range(8):
        whole(kind).wait_send()
    for part in range(PARTS):
        all_sent(part).wait_send()


def gathered_spectra(samples, taps, chan_select):
    vmem = pl.BlockSpec(memory_space=pltpu.VMEM)
    anywhere = pl.BlockSpec(memory_space=pl.ANY)
    return pl.pallas_call(
        spectra_kernel,
        out_shape=[
            jax.ShapeDtypeStruct((8,) + BLOCK, BF16),
            jax.ShapeDtypeStruct((2,) + BLOCK, BF16),
        ],
        in_specs=[vmem, vmem, vmem],
        out_specs=[anywhere, anywhere],
        scratch_shapes=[
            pltpu.VMEM((INPUTS, HALO), BF16),
            pltpu.VMEM((PARTS * HEIGHT, FFT), BF16),
            pltpu.VMEM((PARTS, SHARDS, HEIGHT, LANES), BF16),
            pltpu.VMEM((PARTS, SHARDS, HEIGHT, LANES), BF16),
            pltpu.VMEM((SHARDS * HEIGHT, LANES), F32),
            pltpu.VMEM((GROUP * PART, 2 * DEPTH), F32),
            pltpu.VMEM(BLOCK, BF16),
            pltpu.SemaphoreType.DMA((2,)),
            pltpu.SemaphoreType.DMA((PARTS,)),
            pltpu.SemaphoreType.DMA((PARTS,)),
            pltpu.SemaphoreType.DMA((2,)),
            pltpu.SemaphoreType.DMA((8,)),
            pltpu.SemaphoreType.DMA((8, PARTS)),
        ]
        + [pltpu.VMEM((FFT, 2 * LANES), BF16)] * (SHARDS // 2),
        compiler_params=pltpu.CompilerParams(
            collective_id=0, has_side_effects=True, vmem_limit_bytes=VMEM_LIMIT
        ),
        name="spectra",
    )(samples, taps, chan_select)


CHANNELS = 8
CHUNKS = GROUP // CHANNELS


def cross_kernel(rows, columns, out, products, out_sems):
    sign = jnp.where(lax.broadcasted_iota(jnp.int32, (2 * INPUTS, 2 * DEPTH), 1) < DEPTH, 1.0, -1.0).astype(BF16)

    def store(i):
        channels = pl.ds(i * CHANNELS, CHANNELS)
        return pltpu.make_async_copy(products.at[:, channels], out.at[:, channels], out_sems.at[i])

    def operand(data, c):
        early_and_late = []
        for early in range(2):
            halves = [data[:, 2 * early + half, c] for half in range(2)]
            early_and_late.append(jnp.stack(halves, 1).reshape(-1, 2 * DEPTH))
        return early_and_late

    for i in range(CHUNKS):
        for c in range(i * CHANNELS, (i + 1) * CHANNELS):
            left = operand(rows, c)
            quarter = [jnp.concatenate([block[:, DEPTH:], block[:, :DEPTH]], 1) * sign for block in left]
            left = jnp.concatenate([jnp.concatenate(left, 1), jnp.concatenate(quarter, 1)], 0)
            product = lax.dot_general(
                left, jnp.concatenate(operand(columns, c), 1), (((1,), (1,)), ((), ())),
                preferred_element_type=F32,
            ) * (1.0 / SPECTRA)
            products[:, c] = product.reshape(2, 2, INPUTS, 8 * INPUTS)
        store(i).start()
    for i in range(CHUNKS):
        store(i).wait()


def cross_products(rows, columns):
    shape = (2, GROUP, 2, INPUTS, 8 * INPUTS)
    return pl.pallas_call(
        cross_kernel,
        out_shape=jax.ShapeDtypeStruct(shape, F32),
        in_specs=[pl.BlockSpec(memory_space=pltpu.VMEM)] * 2,
        out_specs=pl.BlockSpec(memory_space=pltpu.HBM),
        scratch_shapes=[pltpu.VMEM(shape, F32), pltpu.SemaphoreType.DMA((CHUNKS,))],
        compiler_params=pltpu.CompilerParams(vmem_limit_bytes=CROSS_LIMIT),
        name="cross",
    )(rows, columns)


def body(samples, pfb_taps, chan_select):
    columns, rows = gathered_spectra(samples[0], pfb_taps, chan_select.reshape(SHARDS // 2, LANES))
    return cross_products(rows, columns)


def solution(mesh):
    return jax.shard_map(
        body,
        mesh=mesh,
        in_specs=(P("grid", "blk", "chan"), P(), P()),
        out_specs=P(None, "chan", None, "blk", "grid"),
        check_vma=False,
    )
```
